512 devices in a mesh: member: 16 (over z), mp: 32 (over x, y, core).
Axes of the slice: x: 4, y: 4, z: 16, core: 2. Of those that a mesh axis runs over, the one named last changes fastest.
Arguments:
- tokens: bfloat16 [16, 64, 64, 1024], P('member', 'mp'), may hold values from -6 to 6
- norm_gain: float32 [1024], replicated, may hold values from 0.5 to 8
- qkv_weight: bfloat16 [1024, 3072], P('mp'), may hold values from -0.1875 to 0.1875
- out_weight: bfloat16 [1024, 1024], P('mp'), may hold values from -0.1875 to 0.1875
- decode_weight: bfloat16 [1024, 90], replicated, may hold values from -0.1875 to 0.1875
- edges: int32 [64, 64, 16], P('mp'), may hold values from 0 to 4095, as said below
- truth: bfloat16 [90, 64, 64], P(None, 'mp', 'member'), may hold values from -6 to 6
Outputs:
- score: float32 [64, 64], P('mp', 'member')
- field_grad: float32 [16, 90, 64, 64], P('member', None, 'mp')
The draws below stay inside these ranges and needn't reach their ends.
Inputs may be any that keep to these rules, and one draw needn't show every extreme that they name: edges[lat, lon, 0] is the node's own index lat * 64 + lon; every other edge of a node in latitude rows of band p (rows p * 2 to (p + 1) * 2 - 1) points to a node of band p - 1, p or p + 1.
All inputs are finite; a program needn't handle non-finite values.
Results may differ from the reference program's by a relative error of at most 0.0062.
The reference program's roundings to bfloat16 on the way (of `normed`, `qkv`, `probs`, `attended` and `fields`) count: a program that leaves them out, or rounds other values in their place, can miss the bound.
Values may be sent and summed in bfloat16 or wider, within the bound.
A program may use at most 64 MiB of HBM per device.

```python
import jax
import jax.numpy as jnp
from jax import lax

D = 1024
HEADS = 16
V = 90
EDGES = 16
HEAD_DIM = 64
MEMBERS = 16
NLAT = 64
NLON = 64
TOK_DEV = 128
N_MP = 32


def draw_norm_gain(key, part):
    key = jax.random.fold_in(key, 11)
    return jax.random.uniform(key, (D,), jnp.float32, 0.5, 1.5)


def draw_edges(key, part):
    key = jax.random.fold_in(key, 23)
    count = NLAT * NLON
    nodes = jnp.arange(count, dtype=jnp.int32)
    band = nodes // TOK_DEV
    low = jnp.maximum(band - 1, 0) * TOK_DEV
    high = jnp.minimum(band + 2, N_MP) * TOK_DEV
    others = jax.random.randint(key, (count, EDGES - 1), low[:, None], high[:, None], jnp.int32)
    table = jnp.concatenate([nodes[:, None], others], axis=1)
    return table.reshape(NLAT, NLON, EDGES)


def block_levels(stream_key, shape, shards, smallest, largest):
    gain, own = 1.0, jax.random.fold_in(stream_key, 6)
    for position, blocks in shards:
        draws = jnp.exp(jax.random.uniform(jax.random.fold_in(own, position), (blocks,), jnp.float32, smallest / len(shards), largest / len(shards)))
        gain = gain * jnp.repeat(draws, shape[position] // blocks).reshape([-1 if axis == position else 1 for axis in range(len(shape))])
    return gain


def bell_draw(key, shape, width, most, shards=(), kind=jnp.bfloat16):
    entries = width * jax.random.normal(key, shape, jnp.float32)
    if shards:
        entries = entries * block_levels(key, shape, shards, -0.22, 0.18)
    return jnp.clip(entries, -most, most).astype(kind)


def setup_inputs(seed: int = 0) -> dict:
    key_of = jax.random.split(jax.random.key(seed), 8)
    return {
        "tokens": bell_draw(key_of[0], (MEMBERS, NLAT, NLON, D), 1.0, 6.0, ((0, 16), (1, 32))),
        "norm_gain": draw_norm_gain(jax.random.fold_in(key_of[7], 71), 0),
        "qkv_weight": bell_draw(key_of[2], (D, 3 * D), D ** -0.5, 0.1875, ((0, 32),)),
        "out_weight": bell_draw(key_of[3], (D, D), D ** -0.5, 0.1875, ((0, 32),)),
        "decode_weight": bell_draw(key_of[4], (D, V), D ** -0.5, 0.1875),
        "edges": draw_edges(jax.random.fold_in(key_of[7], 71), 0),
        "truth": bell_draw(key_of[6], (V, NLAT, NLON), 1.0, 6.0, ((1, 32), (2, 16))),
    }


EPS = 1e-05

def rms_scale(values):
    return values * lax.rsqrt(lax.optimization_barrier(jnp.mean(values * values, axis=-1, keepdims=True)) + 1e-05)

def box_sum(grid):
    rows_sum = grid[..., :-2, :] + grid[..., 1:-1, :] + grid[..., 2:, :]
    return rows_sum[..., :-2] + rows_sum[..., 1:-1] + rows_sum[..., 2:]

def extend(grid):
    lead = [(0, 0)] * (grid.ndim - 2)
    grid = jnp.pad(grid, lead + [(1, 1), (0, 0)])
    return jnp.concatenate([grid[..., -1:], grid, grid[..., :1]], axis=-1)

def member_field(member_tokens, norm_gain, qkv_weight, out_weight, decode_weight, edges):
    count = NLAT * NLON
    states = member_tokens.reshape(count, D).astype(jnp.float32)
    normed = (rms_scale(states) * norm_gain).astype(jnp.bfloat16)
    qkv = jnp.dot(normed, qkv_weight, preferred_element_type=jnp.float32).astype(jnp.bfloat16)
    query = qkv[:, :D]
    keyval = qkv[:, D:]
    flat_edges = edges.reshape(count, EDGES)
    block = 128 if count % 128 == 0 else count

    def attend(args):
        query_block, edge_block = args
        gathered = keyval[edge_block].astype(jnp.float32)
        keys = gathered[..., :D].reshape(block, EDGES, HEADS, HEAD_DIM)
        values = gathered[..., D:].reshape(block, EDGES, HEADS, HEAD_DIM)
        queries = query_block.astype(jnp.float32).reshape(block, HEADS, HEAD_DIM)
        scores = jnp.einsum('bhd,bkhd->bhk', queries, keys) * HEAD_DIM ** (-0.5)
        top = lax.optimization_barrier(jnp.max(scores, axis=-1, keepdims=True))
        expo = jnp.exp(scores - top)
        probs = (expo / lax.optimization_barrier(jnp.sum(expo, axis=-1, keepdims=True))).astype(jnp.bfloat16)
        mixed = jnp.einsum('bhk,bkhd->bhd', probs.astype(jnp.float32), values)
        return mixed.reshape(block, D).astype(jnp.bfloat16)
    attended = lax.map(attend, (query.reshape(count // block, block, D), flat_edges.reshape(count // block, block, EDGES))).reshape(count, D)
    state = states + jnp.dot(attended, out_weight, preferred_element_type=jnp.float32)
    field = jnp.dot(rms_scale(state).astype(jnp.bfloat16), decode_weight, preferred_element_type=jnp.float32).astype(jnp.bfloat16)
    return field.T.reshape(V, NLAT, NLON)

def reference(tokens, norm_gain, qkv_weight, out_weight, decode_weight, edges, truth):
    fields = lax.map(lambda member_tokens: member_field(member_tokens, norm_gain, qkv_weight, out_weight, decode_weight, edges), tokens)
    members = fields.shape[0]
    patch = 9.0 * V
    fields_ext = extend(fields.astype(jnp.float32))
    truth_ext = extend(truth.astype(jnp.float32))
    to_truth = lax.optimization_barrier(jnp.sum((fields_ext - truth_ext[None]) ** 2, axis=1))
    pair = lax.map(lambda row: lax.optimization_barrier(jnp.sum((row[None] - fields_ext) ** 2, axis=1)), fields_ext)
    dist_truth = jnp.sqrt(box_sum(to_truth) / patch + EPS)
    dist_pair = jnp.sqrt(box_sum(pair) / patch + EPS)
    off_diag = (1.0 - jnp.eye(members, dtype=jnp.float32))[:, :, None, None]
    score = lax.optimization_barrier(jnp.mean(dist_truth, axis=0)) - lax.optimization_barrier(jnp.sum(dist_pair * off_diag, axis=(0, 1))) / (2.0 * members * (members - 1))
    coef_truth = 1.0 / dist_truth
    coef_pair = off_diag / ((members - 1) * dist_pair)
    atot = box_sum(extend(coef_truth))
    btot = box_sum(extend(coef_pair))
    centre = fields.astype(jnp.float32)
    truth_c = truth.astype(jnp.float32)

    def one_member(args):
        b_row, a_row, own = args
        return a_row[None] * (own - truth_c) - lax.optimization_barrier(jnp.sum(b_row[:, None] * (own[None] - centre), axis=0))
    field_grad = lax.map(one_member, (btot, atot, centre))
    return (score, field_grad)
```

```python
import jax
import jax.numpy as jnp
from jax import lax
from jax.experimental import pallas as pl
from jax.experimental.pallas import tpu as pltpu
from jax.sharding import PartitionSpec as P

MESH = pl.DeviceIdType.MESH
F32, BF16 = jnp.float32, jnp.bfloat16
EPS = 1e-05
NX, NY, NC = 4, 4, 2
MEMBERS = 16
BANDS = NX * NY * NC
TOK = 128
WIN = 3 * TOK
D = 1024
V = 90
VP = 96
FAN = 16
HEADS_C = 4
QKV_CHUNKS = 4
CHUNKS = QKV_CHUNKS + 1
COLS = 256
STEPS = 17
LANES = MEMBERS * 16
PATCH = 9.0 * V


def iota(shape, dim):
    return lax.broadcasted_iota(jnp.int32, shape, dim)


def hot(mask, dtype=BF16):
    return jnp.where(mask, 1.0, 0.0).astype(dtype)


def dot(a, b, **kw):
    return jnp.dot(a, b, preferred_element_type=F32, **kw)


def dot_t(a, b, **kw):
    return lax.dot_general(a, b, (((1,), (1,)), ((), ())), preferred_element_type=F32, **kw)


def rms_scale(v):
    return v * lax.rsqrt(jnp.mean(v * v, axis=-1, keepdims=True) + EPS)


def kernel(
    tok_ref, gain_ref, wqkv_ref, wout_ref, dec_ref, edge_ref, truth_ref,
    score_ref, grad_ref,
    wq, wo, halo, normed, count, att, stage, recv, trec, e_all, gsend, grecv,
    w_ssem, w_rsem, h_ssem, h_rsem, t_ssem, t_rsem, a_ssem, a_rsem, e_ssem, e_rsem, g_ssem, g_rsem,
):
    z = lax.axis_index("member")
    p = lax.axis_index("mp")
    x, y, c = lax.div(p, NY * NC), lax.rem(lax.div(p, NC), NY), lax.rem(p, NC)
    xm, xp, x2 = lax.rem(x + 3, NX), lax.rem(x + 1, NX), lax.rem(x + 2, NX)
    ym, yp, y2 = lax.rem(y + 3, NY), lax.rem(y + 1, NY), lax.rem(y + 2, NY)

    def chip(cx, cy, cc):
        return (z, (cx * NY + cy) * NC + cc)

    at_xp, at_xm, at_yp, at_ym = chip(xp, y, c), chip(xm, y, c), chip(x, yp, c), chip(x, ym, c)
    sib = chip(x, y, 1 - c)
    low, high = (z, lax.rem(p + BANDS - 1, BANDS)), (z, lax.rem(p + 1, BANDS))

    def other(k):
        return lax.rem(z + k, MEMBERS)

    barrier = pltpu.get_barrier_semaphore()
    partners = [at_xp, at_xm, at_yp, at_ym, sib, low, high]
    for target in partners:
        pl.semaphore_signal(barrier, inc=1, device_id=target, device_id_type=MESH)
    for k in range(1, MEMBERS):
        pl.semaphore_signal(barrier, inc=1, device_id=(other(k), p), device_id_type=MESH)

    for j in range(QKV_CHUNKS):
        for part in range(3):
            wq[j, x, y, c, :, part * COLS : (part + 1) * COLS] = wqkv_ref[
                :, part * D + j * COLS : part * D + (j + 1) * COLS
            ]
    wo[x, y, c] = wout_ref[...]
    pl.semaphore_wait(barrier, len(partners) + MEMBERS - 1)

    sent = []

    def send(src, dst, ssem, rsem, target):
        copy = pltpu.make_async_remote_copy(
            src_ref=src, dst_ref=dst, send_sem=ssem, recv_sem=rsem, device_id=target, device_id_type=MESH
        )
        copy.start()
        sent.append(copy)

    def arrive(dst, ssem, rsem):
        pltpu.make_async_remote_copy(
            src_ref=dst, dst_ref=dst, send_sem=ssem, recv_sem=rsem, device_id=sib, device_id_type=MESH
        ).wait_recv()

    def buf(j):
        return (wq.at[j], 3 * COLS) if j < QKV_CHUNKS else (wo, D)

    A, B = pl.ds(0, 16), pl.ds(16, 16)
    ALL = slice(None)

    def pieces(j):
        _, n = buf(j)
        lo, hi = pl.ds(0, n // 2), pl.ds(n // 2, n // 2)
        return [
            ((x, y, c, A), at_xp, (xm, y, c, A)),
            ((x, y, c, A), at_xm, (xp, y, c, A)),
            ((x, y, c, B), at_yp, (x, ym, c, B)),
            ((x, y, c, B), at_ym, (x, yp, c, B)),
            ((xm, y, c, A, lo), at_xp, (x2, y, c, A, lo)),
            ((xp, y, c, A, hi), at_xm, (x2, y, c, A, hi)),
            ((x, ym, c, B, lo), at_yp, (x, y2, c, B, lo)),
            ((x, yp, c, B, hi), at_ym, (x, y2, c, B, hi)),
            ((ALL, y, c, A), at_yp, (ALL, ym, c, A)),
            ((ALL, y, c, A), at_ym, (ALL, yp, c, A)),
            ((x, ALL, c, B), at_xp, (xm, ALL, c, B)),
            ((x, ALL, c, B), at_xm, (xp, ALL, c, B)),
            ((ALL, ym, c, A, lo), at_yp, (ALL, y2, c, A, lo)),
            ((ALL, yp, c, A, hi), at_ym, (ALL, y2, c, A, hi)),
            ((xm, ALL, c, B, lo), at_xp, (x2, ALL, c, B, lo)),
            ((xp, ALL, c, B, hi), at_xm, (x2, ALL, c, B, hi)),
            ((ALL, ALL, c), sib, (ALL, ALL, 1 - c)),
        ]

    def go(j, first, last):
        ref, _ = buf(j)
        for i in range(first, last):
            src, target, _ = pieces(j)[i]
            send(ref.at[src], ref.at[src], w_ssem.at[j, i], w_rsem.at[j, i], target)

    def got(j, first, last):
        ref, _ = buf(j)
        for i in range(first, last):
            arrive(ref.at[pieces(j)[i][2]], w_ssem.at[j, i], w_rsem.at[j, i])

    go(0, 0, 4)
    send(tok_ref, halo.at[1], h_ssem.at[1], h_rsem.at[1], low)
    send(tok_ref, halo.at[0], h_ssem.at[0], h_rsem.at[0], high)
    for j in range(1, CHUNKS):
        go(j, 0, 4)

    eye90 = hot(iota((V, TOK), 0) == iota((V, TOK), 1))
    truth_t = lax.dot_general(truth_ref[...], eye90, (((0,), (0,)), ((), ())), preferred_element_type=F32)
    trec[1] = jnp.concatenate([truth_t, jnp.zeros_like(truth_t)], axis=0).astype(BF16)
    send(trec.at[1], trec.at[0], t_ssem.at[0], t_rsem.at[0], (other(1), p))
    send(trec.at[1], trec.at[2], t_ssem.at[1], t_rsem.at[1], (other(MEMBERS - 1), p))

    def norm(rows):
        return (rms_scale(rows[...].astype(F32)) * gain_ref[...]).astype(BF16)

    normed[TOK : 2 * TOK] = norm(tok_ref)
    local = edge_ref[...] - (p - 1) * TOK
    nodes = iota((TOK, WIN), 1)
    total = jnp.zeros((TOK, WIN), F32)
    for k in range(FAN):
        total += jnp.where(local[:, k : k + 1] == nodes, 1.0, 0.0)
    count[...] = total

    def heads(j):
        weight = wq[j].reshape(D, 3 * COLS)
        query = dot(normed[TOK : 2 * TOK], weight[:, :COLS]).astype(BF16)
        keyval = dot(normed[...], weight[:, COLS:]).astype(BF16)
        key, value = keyval[:, :COLS], keyval[:, COLS:]
        head_of = iota((TOK, COLS), 1) >> 6
        spread = jnp.concatenate(
            [jnp.where(head_of == h, query, jnp.zeros_like(query)) for h in range(HEADS_C)], axis=0
        )
        scores = dot_t(spread, key) * 0.125
        times = count[...]
        probs = []
        for h in range(HEADS_C):
            s = jnp.where(times > 0.0, scores[h * TOK : (h + 1) * TOK], -1e30)
            expo = jnp.exp(s - jnp.max(s, axis=-1, keepdims=True)) * times
            probs.append((expo * (1.0 / jnp.sum(expo, axis=-1, keepdims=True))).astype(BF16))
        mixed = dot(jnp.concatenate(probs, axis=0), value)
        out = jnp.zeros((TOK, COLS), F32)
        for h in range(HEADS_C):
            out = jnp.where(head_of == h, mixed[h * TOK : (h + 1) * TOK], out)
        att[:, j * COLS : (j + 1) * COLS] = out.astype(BF16)

    for tick in range(CHUNKS + 4):
        j = tick
        if j < CHUNKS:
            got(j, 0, 4)
            go(j, 4, 8)
        j = tick - 1
        if 0 <= j < CHUNKS:
            got(j, 4, 8)
            go(j, 8, 12)
        j = tick - 2
        if 0 <= j < CHUNKS:
            got(j, 8, 12)
            go(j, 12, 16)
        j = tick - 3
        if 0 <= j < CHUNKS:
            got(j, 12, 16)
            go(j, 16, 17)
        if tick == 0:
            arrive(halo.at[0], h_ssem.at[0], h_rsem.at[0])
            arrive(halo.at[1], h_ssem.at[1], h_rsem.at[1])
            normed[:TOK] = norm(halo.at[0])
            normed[2 * TOK :] = norm(halo.at[1])
        j = tick - 4
        if 0 <= j < CHUNKS:
            got(j, 16, 17)
            if j < QKV_CHUNKS:
                heads(j)

    state = tok_ref[...].astype(F32) + dot(att[...], wo[...].reshape(D, D))
    field = dot(rms_scale(state).astype(BF16), dec_ref[...]).astype(BF16)
    field = jnp.concatenate([field, jnp.zeros((TOK, TOK - V), BF16)], axis=1)

    row, col = iota((LANES, TOK), 0), iota((LANES, TOK), 1)
    lon = (4 * (row >> 4) - 2 + (row & 7)) & 63
    pick = hot(col == ((row >> 3) & 1) * 64 + lon)
    stage[...] = dot(pick, field).astype(BF16).reshape(MEMBERS, 16, TOK)
    for k in range(1, MEMBERS):
        send(stage.at[other(k)], recv.at[z], a_ssem.at[k], a_rsem.at[k], (other(k), p))
    recv[z] = stage[z]

    arrive(trec.at[0], t_ssem.at[0], t_rsem.at[0])
    arrive(trec.at[2], t_ssem.at[1], t_rsem.at[1])
    row, col = iota((LANES, 48), 0), iota((LANES, 48), 1)
    spot = (row & 7) + 2
    source = (spot >> 2) * 16 + ((row >> 3) & 1) * 4 + (spot & 3)
    truth_rows = dot(hot(col == source), trec[...].reshape(48, TOK)).astype(BF16)
    eye = hot(iota((VP, TOK), 0) == iota((VP, TOK), 1))
    truth_f = dot_t(eye, truth_rows)

    for k in range(1, MEMBERS):
        arrive(recv.at[other(MEMBERS - k)], a_ssem.at[k], a_rsem.at[k])
    fields = dot_t(eye, recv[...].reshape(LANES, TOK))

    def shifted(grid, k):
        return pltpu.roll(grid, (LANES - 16 * k) % LANES, axis=1)

    def row_sum(grid):
        return jnp.sum(grid * grid, axis=0, keepdims=True)

    e_all[1, 0:1] = row_sum(fields - truth_f)
    for k in range(1, MEMBERS // 2 + 1):
        e_k = row_sum(fields - shifted(fields, k))
        e_all[1, k : k + 1] = e_k
        if k < MEMBERS // 2:
            e_all[1, MEMBERS - k : MEMBERS - k + 1] = shifted(e_k, MEMBERS - k)

    send(e_all.at[1], e_all.at[0], e_ssem.at[0], e_rsem.at[0], high)
    send(e_all.at[1], e_all.at[2], e_ssem.at[1], e_rsem.at[1], low)
    arrive(e_all.at[0], e_ssem.at[0], e_rsem.at[0])
    arrive(e_all.at[2], e_ssem.at[1], e_rsem.at[1])

    lane = iota((MEMBERS, LANES), 1)
    north = ((lane >> 3) & 1) == 0
    below = jnp.where(p > 0, 1.0, 0.0)
    above = jnp.where(p < BANDS - 1, 1.0, 0.0)

    def swap(grid):
        return jnp.where(north, pltpu.roll(grid, LANES - 8, axis=1), pltpu.roll(grid, 8, axis=1))

    def along(grid):
        return pltpu.roll(grid, 1, axis=1) + grid + pltpu.roll(grid, LANES - 1, axis=1)

    e_low, e_own, e_high = e_all[0] * below, e_all[1], e_all[2] * above
    s_low, s_own, s_high = swap(e_low), swap(e_own), swap(e_high)
    box_own = along(e_own + s_own + jnp.where(north, s_low, s_high))
    box_out = along(s_own + jnp.where(north, e_high + s_high, e_low + s_low))
    d_own = jnp.sqrt(box_own / PATCH + EPS)
    d_out = jnp.sqrt(box_out / PATCH + EPS)
    first = iota((MEMBERS, LANES), 0) == 0
    scale = jnp.where(first, 1.0, 1.0 / (MEMBERS - 1))
    c_own = scale / d_own
    c_out = scale / d_out * jnp.where(north, above, below)
    btot = along(c_own + swap(c_own) + swap(c_out))

    part = jnp.sum(d_own * jnp.where(first, 1.0 / MEMBERS, -0.5 / (MEMBERS * (MEMBERS - 1))), axis=0, keepdims=True)
    for shift in (128, 64, 32, 16):
        part = part + pltpu.roll(part, shift, axis=1)
    score_ref[0:1] = part[:, 2:6]
    score_ref[1:2] = part[:, 10:14]

    grad = btot[0:1] * (fields - truth_f)
    for k in range(1, MEMBERS):
        grad = grad - btot[k : k + 1] * (fields - shifted(fields, k))
    grad = jnp.concatenate([grad, jnp.zeros((TOK - VP, LANES), F32)], axis=0)
    row, col = iota((TOK, LANES), 0), iota((TOK, LANES), 1)
    pick = hot(col == (row >> 3) * 16 + ((row >> 2) & 1) * 8 + 2 + (row & 3), F32)
    gsend[...] = dot_t(pick, grad, precision=lax.Precision.HIGHEST).reshape(MEMBERS, 8, TOK)
    for k in range(1, MEMBERS):
        send(gsend.at[other(k)], grecv.at[z], g_ssem.at[k], g_rsem.at[k], (other(k), p))
    grecv[z] = gsend[z]
    row, col = iota((TOK, TOK), 0), iota((TOK, TOK), 1)
    pick = hot(col == ((row & 63) >> 2) * 8 + (row >> 6) * 4 + (row & 3), F32)
    for k in range(1, MEMBERS):
        arrive(grecv.at[other(MEMBERS - k)], g_ssem.at[k], g_rsem.at[k])
    cells = dot(pick, grecv[...].reshape(TOK, TOK), precision=lax.Precision.HIGHEST)
    grad_ref[...] = cells.T[:V]
    for copy in sent:
        copy.wait_send()


def on_device(tokens, norm_gain, qkv_weight, out_weight, decode_weight, edges, truth):
    vmem = pl.BlockSpec(memory_space=pltpu.VMEM)
    dma = pltpu.SemaphoreType.DMA
    score, grad = pl.pallas_call(
        kernel,
        out_shape=(jax.ShapeDtypeStruct((2, 4), F32), jax.ShapeDtypeStruct((V, TOK), F32)),
        in_specs=[vmem] * 7,
        out_specs=(vmem, vmem),
        scratch_shapes=[
            pltpu.VMEM((QKV_CHUNKS, NX, NY, NC, 32, 3 * COLS), BF16),
            pltpu.VMEM((NX, NY, NC, 32, D), BF16),
            pltpu.VMEM((2, TOK, D), BF16),
            pltpu.VMEM((WIN, D), BF16),
            pltpu.VMEM((TOK, WIN), F32),
            pltpu.VMEM((TOK, D), BF16),
            pltpu.VMEM((MEMBERS, 16, TOK), BF16),
            pltpu.VMEM((MEMBERS, 16, TOK), BF16),
            pltpu.VMEM((3, 16, TOK), BF16),
            pltpu.VMEM((3, MEMBERS, LANES), F32),
            pltpu.VMEM((MEMBERS, 8, TOK), F32),
            pltpu.VMEM((MEMBERS, 8, TOK), F32),
            dma((CHUNKS, STEPS)),
            dma((CHUNKS, STEPS)),
            dma((2,)),
            dma((2,)),
            dma((2,)),
            dma((2,)),
            dma((MEMBERS,)),
            dma((MEMBERS,)),
            dma((2,)),
            dma((2,)),
            dma((MEMBERS,)),
            dma((MEMBERS,)),
        ],
        compiler_params=pltpu.CompilerParams(
            collective_id=0, has_side_effects=True, vmem_limit_bytes=48 * 1024 * 1024
        ),
    )(
        tokens.reshape(TOK, D),
        norm_gain.reshape(1, D),
        qkv_weight,
        out_weight,
        decode_weight,
        edges.reshape(TOK, FAN),
        truth.reshape(V, 8),
    )
    return score, grad.reshape(1, V, 2, 64)


def solution(mesh):
    in_specs = (
        P("member", "mp", None, None),
        P(),
        P("mp", None),
        P("mp", None),
        P(),
        P("mp", None, None),
        P(None, "mp", "member"),
    )
    out_specs = (P("mp", "member"), P("member", None, "mp", None))
    return jax.shard_map(on_device, mesh=mesh, in_specs=in_specs, out_specs=out_specs, check_vma=False)
```

```python
import jax
import jax.numpy as jnp
from jax import lax
from jax.experimental import pallas as pl
from jax.experimental.pallas import tpu as pltpu
from jax.sharding import PartitionSpec as P

MESH = pl.DeviceIdType.MESH
F32, BF16 = jnp.float32, jnp.bfloat16
EPS = 1e-05
NX, NY, NC = 4, 4, 2
MEMBERS = 16
BANDS = NX * NY * NC
TOK = 128
WIN = 3 * TOK
D = 1024
V = 90
VP = 96
FAN = 16
HEADS_C = 4
QKV_CHUNKS = 4
OUT_CHUNKS = 2
CHUNKS = QKV_CHUNKS + OUT_CHUNKS
COLS = 256
OUT_COLS = D // OUT_CHUNKS
STEPS = 33
REACH = 4
HALF = VP // 2
TILE = MEMBERS * 16
PATCH = 9.0 * V
FAR_FIRST, FAR_SECOND = (0,), (CHUNKS - 1,)
PAIRS = {0: 1}
ORDER = (
    ("first", 0), ("relay", 2), ("halo", 0), ("relay", 3), ("relay", 4), ("relay", 5), ("second", 2), ("again", 0),
    ("second", 3), ("core", 0), ("again", 2), ("second", 4), ("truth", 0), ("done", 0), ("heads", 0), ("again", 3),
    ("core", 2), ("second", 5), ("core", 1), ("done", 2), ("heads", 2), ("again", 4), ("core", 3), ("done", 1),
    ("heads", 1), ("core", 4), ("core", 5), ("done", 3), ("heads", 3), ("done", 4), ("out", 4), ("done", 5),
    ("out", 5),
)


def iota(shape, dim):
    return lax.broadcasted_iota(jnp.int32, shape, dim)


def hot(mask, dtype=BF16):
    return jnp.where(mask, 1.0, 0.0).astype(dtype)


def dot(a, b, **kw):
    return jnp.dot(a, b, preferred_element_type=F32, **kw)


def dot_t(a, b, **kw):
    return lax.dot_general(a, b, (((1,), (1,)), ((), ())), preferred_element_type=F32, **kw)


def rms_scale(v):
    return v * lax.rsqrt(jnp.mean(v * v, axis=-1, keepdims=True) + EPS)


def kernel(
    tok_hbm, gain_hbm, wqkv_hbm, wout_hbm, dec_hbm, edge_hbm, truth_hbm,
    score_ref, grad_ref,
    tok_ref, gain_ref, dec_ref, edge_ref, truth_ref, wq, wo, halo, normed, count, att, state, dec, truths, fields, pick, e_all,
    in_sem, w_ssem, w_rsem, h_ssem, h_rsem, t_ssem, t_rsem, f_ssem, f_rsem, e_ssem, e_rsem,
):
    z = lax.axis_index("member")
    p = lax.axis_index("mp")
    x, y, c = lax.div(p, NY * NC), lax.rem(lax.div(p, NC), NY), lax.rem(p, NC)
    xm, xp, x2 = lax.rem(x + 3, NX), lax.rem(x + 1, NX), lax.rem(x + 2, NX)
    ym, yp, y2 = lax.rem(y + 3, NY), lax.rem(y + 1, NY), lax.rem(y + 2, NY)

    def chip(cx, cy, cc):
        return (z, (cx * NY + cy) * NC + cc)

    odd = lax.rem(z, 2)

    def columns(j, size):
        first = QKV_CHUNKS if j >= QKV_CHUNKS else 0
        if j in PAIRS:
            return pl.multiple_of((j - first + odd) * size, size)
        if j in PAIRS.values():
            return pl.multiple_of((j - first - odd) * size, size)
        return (j - first) * size

    at_xp, at_xm, at_yp, at_ym = chip(xp, y, c), chip(xm, y, c), chip(x, yp, c), chip(x, ym, c)
    at_x2, at_y2 = chip(x2, y, c), chip(x, y2, c)
    sib = chip(x, y, 1 - c)
    low, high = (z, lax.rem(p + BANDS - 1, BANDS)), (z, lax.rem(p + 1, BANDS))

    def other(k):
        return lax.rem(z + (k + MEMBERS), MEMBERS)

    barrier = pltpu.get_barrier_semaphore()
    partners = [at_xp, at_xm, at_yp, at_ym, at_x2, at_y2, sib, low, high]
    partners += [(other(k), p) for k in range(-REACH, REACH + 1) if k]
    for target in partners:
        pl.semaphore_signal(barrier, inc=1, device_id=target, device_id_type=MESH)

    loads = []

    def load(src, dst):
        copy = pltpu.make_async_copy(src, dst, in_sem.at[len(loads)])
        copy.start()
        loads.append(copy)

    gathered = [j for j in range(CHUNKS) if j not in PAIRS.values()]
    for j in gathered:
        if j < QKV_CHUNKS:
            for part in range(3):
                load(
                    wqkv_hbm.at[:, pl.ds(part * D + columns(j, COLS), COLS)],
                    wq.at[j, x, y, c, :, pl.ds(part * COLS, COLS)],
                )
        else:
            load(wout_hbm.at[:, pl.ds(columns(j, OUT_COLS), OUT_COLS)], wo.at[j - QKV_CHUNKS, x, y, c])
    weight_loads = len(loads)
    small = ((truth_hbm, truth_ref), (gain_hbm, gain_ref), (edge_hbm, edge_ref), (dec_hbm, dec_ref))
    for src, dst in ((tok_hbm, tok_ref),) + small:
        load(src, dst)
    for copy in loads[: weight_loads + 2]:
        copy.wait()
    cells = jnp.concatenate([truth_ref[0], truth_ref[1], jnp.zeros((8, V), BF16)], axis=0)
    truths[z] = jnp.concatenate([cells, jnp.zeros((16, TOK - V), BF16)], axis=1)
    pl.semaphore_wait(barrier, len(partners))

    sent = []

    def send(src, dst, ssem, rsem, target):
        copy = pltpu.make_async_remote_copy(
            src_ref=src, dst_ref=dst, send_sem=ssem, recv_sem=rsem, device_id=target, device_id_type=MESH
        )
        copy.start()
        sent.append(copy)

    def arrive(dst, ssem, rsem):
        pltpu.make_async_remote_copy(
            src_ref=dst, dst_ref=dst, send_sem=ssem, recv_sem=rsem, device_id=sib, device_id_type=MESH
        ).wait_recv()

    def buf(j):
        return (wq.at[j], 3 * COLS) if j < QKV_CHUNKS else (wo.at[j - QKV_CHUNKS], OUT_COLS)

    A, B = pl.ds(0, 16), pl.ds(16, 16)
    ALL = slice(None)

    def pieces(j, step):
        _, n = buf(j)
        lo, hi = pl.ds(0, n // 2), pl.ds(n // 2, n // 2)
        if step == "start":
            near = [
                (0, (x, y, c, A), at_xp, (xm, y, c, A)),
                (1, (x, y, c, A), at_xm, (xp, y, c, A)),
                (2, (x, y, c, B), at_yp, (x, ym, c, B)),
                (3, (x, y, c, B), at_ym, (x, yp, c, B)),
            ]
            far = [(4, (x, y, c, A), at_x2, (x2, y, c, A)), (6, (x, y, c, B), at_y2, (x, y2, c, B))]
            return near + far if j in FAR_FIRST else near
        if step == "relay":
            return [
                (4, (xm, y, c, A, lo), at_xp, (x2, y, c, A, lo)),
                (5, (xp, y, c, A, hi), at_xm, (x2, y, c, A, hi)),
                (6, (x, ym, c, B, lo), at_yp, (x, y2, c, B, lo)),
                (7, (x, yp, c, B, hi), at_ym, (x, y2, c, B, hi)),
            ]
        if step == "second":
            near = [
                (8, (ALL, y, c, A), at_yp, (ALL, ym, c, A)),
                (9, (ALL, y, c, A), at_ym, (ALL, yp, c, A)),
                (10, (x, ALL, c, B), at_xp, (xm, ALL, c, B)),
                (11, (x, ALL, c, B), at_xm, (xp, ALL, c, B)),
            ]
            far = [(12, (ALL, y, c, A), at_y2, (ALL, y2, c, A)), (14, (x, ALL, c, B), at_x2, (x2, ALL, c, B))]
            return far + near if j in FAR_SECOND else near
        if step == "again":
            return [
                (12, (ALL, ym, c, A, lo), at_yp, (ALL, y2, c, A, lo)),
                (13, (ALL, yp, c, A, hi), at_ym, (ALL, y2, c, A, hi)),
                (14, (xm, ALL, c, B, lo), at_xp, (x2, ALL, c, B, lo)),
                (15, (xp, ALL, c, B, hi), at_xm, (x2, ALL, c, B, hi)),
            ]
        if step == "core_near":
            return [(16, (ALL, y, c, A), sib, (ALL, y, 1 - c, A)), (17, (x, ALL, c, B), sib, (x, ALL, 1 - c, B))]
        if step == "core_next":
            return [
                (18, (ALL, ym, c, A), sib, (ALL, ym, 1 - c, A)),
                (19, (ALL, yp, c, A), sib, (ALL, yp, 1 - c, A)),
                (20, (xm, ALL, c, B), sib, (xm, ALL, 1 - c, B)),
                (21, (xp, ALL, c, B), sib, (xp, ALL, 1 - c, B)),
            ]
        return [(22, (ALL, y2, c, A), sib, (ALL, y2, 1 - c, A)), (23, (x2, ALL, c, B), sib, (x2, ALL, 1 - c, B))]

    def go(j, step):
        ref, _ = buf(j)
        for i, src, target, _ in pieces(j, step):
            send(ref.at[src], ref.at[src], w_ssem.at[j, i], w_rsem.at[j, i], target)

    def got(j, *steps):
        ref, _ = buf(j)
        for step in steps:
            for i, _, _, dst in pieces(j, step):
                arrive(ref.at[dst], w_ssem.at[j, i], w_rsem.at[j, i])

    up, down = (other(1), p), (other(-1), p)
    Z_NEAR = [
        (24, (ALL, ym, c, A), up), (25, (ALL, y, c, A), up), (26, (ALL, yp, c, A), up),
        (27, (xm, ALL, c, B), down), (28, (x, ALL, c, B), down), (29, (xp, ALL, c, B), down),
    ]
    Z_LAST = [(30, (ALL, y2, c, A), up), (31, (x2, ALL, c, B), down)]

    def go_z(j, part):
        if j in PAIRS:
            mine, theirs, k = buf(j)[0], buf(PAIRS[j])[0], PAIRS[j]
            for i, where, target in part:
                send(mine.at[where], theirs.at[where], w_ssem.at[k, i], w_rsem.at[k, i], target)

    def reach(ref, ssem, rsem):
        for d in range(REACH, 0, -1):
            send(ref.at[z], ref.at[z], ssem.at[d], rsem.at[d], (other(d), p))
            send(ref.at[z], ref.at[z], ssem.at[REACH + d], rsem.at[REACH + d], (other(-d), p))

    def relay(ref, ssem, rsem):
        behind, ahead = ref.at[other(-REACH)], ref.at[other(REACH)]
        arrive(behind, ssem.at[REACH], rsem.at[REACH])
        arrive(ahead, ssem.at[2 * REACH], rsem.at[2 * REACH])
        rows = ref.shape[1] // 2
        if rows % 16 == 0:
            first, second = pl.ds(0, rows), pl.ds(rows, rows)
            send(behind.at[first], behind.at[first], ssem.at[12], rsem.at[12], (other(REACH), p))
            send(ahead.at[second], ahead.at[second], ssem.at[16], rsem.at[16], (other(-REACH), p))
        else:
            send(behind, behind, ssem.at[12], rsem.at[12], (other(REACH), p))
        for d in range(REACH - 1, 0, -1):
            send(behind, behind, ssem.at[8 + d], rsem.at[8 + d], (other(d), p))
            send(ahead, ahead, ssem.at[12 + d], rsem.at[12 + d], (other(-d), p))

    def reached(ref, ssem, rsem):
        for d in range(1, REACH):
            arrive(ref.at[other(-d)], ssem.at[d], rsem.at[d])
            arrive(ref.at[other(d)], ssem.at[REACH + d], rsem.at[REACH + d])
        for d in range(1, REACH):
            arrive(ref.at[other(-REACH - d)], ssem.at[8 + d], rsem.at[8 + d])
            arrive(ref.at[other(REACH + d)], ssem.at[12 + d], rsem.at[12 + d])
        opposite = ref.at[other(MEMBERS // 2)]
        rows = ref.shape[1] // 2
        if rows % 16 == 0:
            arrive(opposite.at[pl.ds(0, rows)], ssem.at[12], rsem.at[12])
            arrive(opposite.at[pl.ds(rows, rows)], ssem.at[16], rsem.at[16])
        else:
            arrive(opposite, ssem.at[12], rsem.at[12])

    go(0, "start")
    for j in gathered[1:]:
        go(j, "start")
    reach(truths, t_ssem, t_rsem)

    def norm(rows):
        return (rms_scale(rows[...].astype(F32)) * gain_ref[...]).astype(BF16)

    for copy in loads[weight_loads + 2 :]:
        copy.wait()
    normed[TOK : 2 * TOK] = norm(tok_ref)
    local = jnp.concatenate([edge_ref[0], edge_ref[1]], axis=1) - (p - 1) * TOK
    nodes = iota((WIN, TOK), 0)
    total = jnp.zeros((WIN, TOK), F32)
    for k in range(FAN):
        total += jnp.where(local[k : k + 1] == nodes, 1.0, 0.0)
    count[...] = total.T
    dec[...] = jnp.zeros_like(dec)
    dec[:V] = dec_ref[...]
    row, col = iota((MEMBERS * TOK, TILE), 0), iota((MEMBERS * TOK, TILE), 1)
    cell = ((col >> 3) & 1) * 64 + ((4 * z - 2 + (col & 7)) & 63)
    pick[...] = hot(row == (col >> 4) * TOK + cell)

    def heads(j):
        weight = wq[j].reshape(D, 3 * COLS)
        query = dot(normed[TOK : 2 * TOK], weight[:, :COLS]).astype(BF16)
        keyval = dot(normed[...], weight[:, COLS:]).astype(BF16)
        key, value = keyval[:, :COLS], keyval[:, COLS:]
        head_of = iota((TOK, COLS), 1) >> 6
        spread = jnp.concatenate(
            [jnp.where(head_of == h, query, jnp.zeros_like(query)) for h in range(HEADS_C)], axis=0
        )
        scores = dot_t(spread, key) * 0.125
        times = count[...]
        probs = []
        for h in range(HEADS_C):
            s = jnp.where(times > 0.0, scores[h * TOK : (h + 1) * TOK], -1e30)
            expo = jnp.exp(s - jnp.max(s, axis=-1, keepdims=True)) * times
            probs.append((expo * (1.0 / jnp.sum(expo, axis=-1, keepdims=True))).astype(BF16))
        mixed = dot(jnp.concatenate(probs, axis=0), value)
        out = jnp.zeros((TOK, COLS), F32)
        for h in range(HEADS_C):
            out = jnp.where(head_of == h, mixed[h * TOK : (h + 1) * TOK], out)
        att[:, pl.ds(columns(j, COLS), COLS)] = out.astype(BF16)

    def project(j):
        i = j - QKV_CHUNKS
        where = pl.ds(columns(j, OUT_COLS), OUT_COLS)
        state[:, where] = tok_ref[:, where].astype(F32) + dot(att[...], wo[i].reshape(D, OUT_COLS))

    for step, j in ORDER:
        if step == "halo":
            send(tok_ref, halo.at[1], h_ssem.at[1], h_rsem.at[1], low)
            send(tok_ref, halo.at[0], h_ssem.at[0], h_rsem.at[0], high)
            continue
        if step == "truth":
            relay(truths, t_ssem, t_rsem)
            continue
        if step == "first":
            got(j, "start")
            go(j, "second")
            go(j, "core_near")
        elif step == "relay":
            got(j, "start")
            go(j, "relay")
        elif step == "second":
            got(j, "relay")
            go(j, "second")
            go(j, "core_near")
        elif step == "again":
            got(j, "second")
            go_z(j, Z_NEAR)
            go(j, "again")
            go(j, "core_next")
        elif step == "core" and j in PAIRS.values():
            ref = buf(j)[0]
            for i, where, _ in Z_NEAR + Z_LAST:
                arrive(ref.at[where], w_ssem.at[j, i], w_rsem.at[j, i])
            send(ref.at[ALL, ALL, c], ref.at[ALL, ALL, c], w_ssem.at[j, 32], w_rsem.at[j, 32], sib)
        elif step == "core":
            if j in FAR_SECOND:
                got(j, "second")
                go(j, "core_next")
            else:
                got(j, "again")
            go_z(j, Z_LAST)
            go(j, "core_last")
        elif step == "done" and j in PAIRS.values():
            arrive(buf(j)[0].at[ALL, ALL, 1 - c], w_ssem.at[j, 32], w_rsem.at[j, 32])
        elif step == "done":
            got(j, "core_near", "core_next", "core_last")
        elif step == "out":
            project(j)
        elif step == "heads":
            if j == 0:
                arrive(halo.at[0], h_ssem.at[0], h_rsem.at[0])
                arrive(halo.at[1], h_ssem.at[1], h_rsem.at[1])
                normed[:TOK] = norm(halo.at[0])
                normed[2 * TOK :] = norm(halo.at[1])
            heads(j)

    fields[z] = dot_t(dec[...], rms_scale(state[...]).astype(BF16)).astype(BF16)
    reach(fields, f_ssem, f_rsem)

    reached(truths, t_ssem, t_rsem)
    row, col = iota((TOK, TILE), 0), iota((TOK, TILE), 1)
    source = ((row & 63) >> 2) * 16 + (row >> 6) * 4 + (row & 3)
    truth_rows = dot(hot(col == source), truths[...].reshape(TILE, TOK)).astype(BF16)
    eye = hot(iota((VP, TOK), 0) == iota((VP, TOK), 1))
    truth_b = dot_t(eye, truth_rows)
    spot = ((col >> 3) & 1) * 64 + ((4 * z - 2 + (col & 7)) & 63)
    truth_tile = dot(truth_b.astype(BF16), hot(row == spot))
    own = fields[z].astype(F32)

    relay(fields, f_ssem, f_rsem)
    reached(fields, f_ssem, f_rsem)

    def row_sum(grid):
        return jnp.sum(grid * grid, axis=0, keepdims=True)

    e_all[1, 0:1, :TOK] = row_sum(own - truth_b)
    for k in range(1, MEMBERS):
        e_all[1, k : k + 1, :TOK] = row_sum(own - fields[other(k)].astype(F32))
    tile = dot(jnp.concatenate([fields[m] for m in range(MEMBERS)], axis=1), pick[...])
    e_all[1, 8:16, TOK:] = jnp.zeros((8, TILE), F32)
    e_all[1, 0:1, TOK:] = row_sum(tile - truth_tile)
    for k in range(1, MEMBERS // 2 + 1):
        e_all[1, k : k + 1, TOK:] = row_sum(tile - pltpu.roll(tile, TILE - 16 * k, axis=1))

    send(e_all.at[1], e_all.at[0], e_ssem.at[0], e_rsem.at[0], high)
    send(e_all.at[1], e_all.at[2], e_ssem.at[1], e_rsem.at[1], low)
    arrive(e_all.at[0], e_ssem.at[0], e_rsem.at[0])
    arrive(e_all.at[2], e_ssem.at[1], e_rsem.at[1])

    below = jnp.where(p > 0, 1.0, 0.0)
    above = jnp.where(p < BANDS - 1, 1.0, 0.0)
    e_low, e_own, e_high = e_all[0] * below, e_all[1], e_all[2] * above

    lane = iota((MEMBERS, TOK), 1)
    north, lon = lane < 64, lane & 63

    def swap(grid):
        return pltpu.roll(grid, 64, axis=1)

    def along(grid):
        west = jnp.where(lon == 0, pltpu.roll(grid, 65, axis=1), pltpu.roll(grid, 1, axis=1))
        east = jnp.where(lon == 63, pltpu.roll(grid, 63, axis=1), pltpu.roll(grid, TOK - 1, axis=1))
        return west + grid + east

    r_low, r_own, r_high = e_low[:, :TOK], e_own[:, :TOK], e_high[:, :TOK]
    s_low, s_own, s_high = swap(r_low), swap(r_own), swap(r_high)
    box_own = along(r_own + s_own + jnp.where(north, s_low, s_high))
    box_out = along(s_own + jnp.where(north, r_high + s_high, r_low + s_low))
    scale = jnp.where(iota((MEMBERS, TOK), 0) == 0, 1.0, 1.0 / (MEMBERS - 1))
    c_own = scale / jnp.sqrt(box_own / PATCH + EPS)
    c_out = scale / jnp.sqrt(box_out / PATCH + EPS) * jnp.where(north, above, below)
    btot = along(c_own + swap(c_own) + swap(c_out))
    grad = btot[0:1] * (own - truth_b)
    for k in range(1, MEMBERS):
        grad = grad - btot[k : k + 1] * (own - fields[other(k)].astype(F32))
    grad_ref[...] = grad[:V]

    lane = iota((MEMBERS, TILE), 1)
    north = ((lane >> 3) & 1) == 0

    def swap_tile(grid):
        return jnp.where(north, pltpu.roll(grid, TILE - 8, axis=1), pltpu.roll(grid, 8, axis=1))

    t_own = e_own[:, TOK:]
    rows = t_own + swap_tile(t_own) + jnp.where(north, swap_tile(e_low[:, TOK:]), swap_tile(e_high[:, TOK:]))
    box = pltpu.roll(rows, 1, axis=1) + rows + pltpu.roll(rows, TILE - 1, axis=1)
    apart = iota((MEMBERS, TILE), 0)
    pair = 0.5 / (MEMBERS * (MEMBERS - 1))
    weight = jnp.where(apart == 0, 1.0 / MEMBERS, jnp.where(apart < MEMBERS // 2, -2.0 * pair, -pair))
    weight = jnp.where(apart > MEMBERS // 2, 0.0, weight)
    part = jnp.sum(jnp.sqrt(box / PATCH + EPS) * weight, axis=0, keepdims=True)
    for shift in (128, 64, 32, 16):
        part = part + pltpu.roll(part, shift, axis=1)
    score_ref[0:1] = part[:, 2:6]
    score_ref[1:2] = part[:, 10:14]
    for copy in sent:
        copy.wait_send()


def on_device(tokens, norm_gain, qkv_weight, out_weight, decode_weight, edges, truth):
    vmem = pl.BlockSpec(memory_space=pltpu.VMEM)
    dma = pltpu.SemaphoreType.DMA
    score, grad = pl.pallas_call(
        kernel,
        out_shape=(jax.ShapeDtypeStruct((2, 4), F32), jax.ShapeDtypeStruct((V, TOK), F32)),
        in_specs=[pl.BlockSpec(memory_space=pltpu.HBM)] * 7,
        out_specs=(vmem, vmem),
        scratch_shapes=[
            pltpu.VMEM((TOK, D), BF16),
            pltpu.VMEM((1, D), F32),
            pltpu.VMEM((V, D), BF16),
            pltpu.VMEM((2, FAN, 64), jnp.int32),
            pltpu.VMEM((2, 4, V), BF16),
            pltpu.VMEM((QKV_CHUNKS, NX, NY, NC, 32, 3 * COLS), BF16),
            pltpu.VMEM((OUT_CHUNKS, NX, NY, NC, 32, OUT_COLS), BF16),
            pltpu.VMEM((2, TOK, D), BF16),
            pltpu.VMEM((WIN, D), BF16),
            pltpu.VMEM((TOK, WIN), F32),
            pltpu.VMEM((TOK, D), BF16),
            pltpu.VMEM((TOK, D), F32),
            pltpu.VMEM((VP, D), BF16),
            pltpu.VMEM((MEMBERS, 16, TOK), BF16),
            pltpu.VMEM((MEMBERS, VP, TOK), BF16),
            pltpu.VMEM((MEMBERS * TOK, TILE), BF16),
            pltpu.VMEM((3, MEMBERS, TOK + TILE), F32),
            dma((3 * QKV_CHUNKS + OUT_CHUNKS + 5,)),
            dma((CHUNKS, STEPS)),
            dma((CHUNKS, STEPS)),
            dma((2,)),
            dma((2,)),
            dma((4 * REACH + 1,)),
            dma((4 * REACH + 1,)),
            dma((4 * REACH + 1,)),
            dma((4 * REACH + 1,)),
            dma((2,)),
            dma((2,)),
        ],
        compiler_params=pltpu.CompilerParams(
            collective_id=0, has_side_effects=True, vmem_limit_bytes=48 * 1024 * 1024
        ),
    )(
        *(pltpu.with_memory_space_constraint(a, pltpu.HBM) for a in (
            tokens.reshape(TOK, D),
            norm_gain.reshape(1, D),
            qkv_weight,
            out_weight,
            decode_weight.T,
            edges.transpose(0, 2, 1),
            truth.transpose(1, 2, 0),
        ))
    )
    return score, grad.reshape(1, V, 2, 64)


def solution(mesh):
    in_specs = (
        P("member", "mp", None, None),
        P(),
        P("mp", None),
        P("mp", None),
        P(),
        P("mp", None, None),
        P(None, "mp", "member"),
    )
    out_specs = (P("mp", "member"), P("member", None, "mp", None))
    return jax.shard_map(on_device, mesh=mesh, in_specs=in_specs, out_specs=out_specs, check_vma=False)
```

```python
import jax
import jax.numpy as jnp
from jax import lax
from jax.experimental import pallas as pl
from jax.experimental.pallas import tpu as pltpu
from jax.sharding import PartitionSpec as P

MESH = pl.DeviceIdType.MESH
F32, BF16 = jnp.float32, jnp.bfloat16
EPS = 1e-05
NX, NY, NC = 4, 4, 2
MEMBERS = 16
BANDS = NX * NY * NC
TOK = 128
WIN = 3 * TOK
D = 1024
V = 90
VP = 96
FAN = 16
HEADS_C = 4
QKV_CHUNKS = 4
OUT_CHUNKS = 2
CHUNKS = QKV_CHUNKS + OUT_CHUNKS
COLS = 256
OUT_COLS = D // OUT_CHUNKS
STEPS = 33
REACH = 4
HALF = VP // 2
TILE = MEMBERS * 16
PATCH = 9.0 * V
FAR_FIRST, FAR_SECOND = (0, 2, 3), (CHUNKS - 1,)
PAIRS = {0: 1}
ORDER = (
    ("first", 0), ("first", 2), ("first", 3), ("relay", 4), ("relay", 5), ("again", 0), ("halo", 0), ("again", 2),
    ("core", 0), ("second", 4), ("again", 3), ("second", 5), ("core", 2), ("truth", 0), ("done", 0), ("heads", 0),
    ("core", 1), ("again", 4), ("core", 3), ("done", 2), ("heads", 2), ("done", 1), ("heads", 1), ("core", 4),
    ("core", 5), ("done", 3), ("heads", 3), ("done", 4), ("out", 4), ("done", 5), ("out", 5),
)


def iota(shape, dim):
    return lax.broadcasted_iota(jnp.int32, shape, dim)


def hot(mask, dtype=BF16):
    return jnp.where(mask, 1.0, 0.0).astype(dtype)


def dot(a, b, **kw):
    return jnp.dot(a, b, preferred_element_type=F32, **kw)


def dot_t(a, b, **kw):
    return lax.dot_general(a, b, (((1,), (1,)), ((), ())), preferred_element_type=F32, **kw)


def rms_scale(v):
    return v * lax.rsqrt(jnp.mean(v * v, axis=-1, keepdims=True) + EPS)


def kernel(
    tok_hbm, gain_hbm, wqkv_hbm, wout_hbm, dec_hbm, edge_hbm, truth_hbm,
    score_ref, grad_ref,
    tok_ref, gain_ref, dec_ref, edge_ref, truth_ref, wq, wo, halo, normed, count, att, state, dec, truths, fields, pick, e_all,
    in_sem, w_ssem, w_rsem, h_ssem, h_rsem, t_ssem, t_rsem, f_ssem, f_rsem, e_ssem, e_rsem,
):
    z = lax.axis_index("member")
    p = lax.axis_index("mp")
    x, y, c = lax.div(p, NY * NC), lax.rem(lax.div(p, NC), NY), lax.rem(p, NC)
    xm, xp, x2 = lax.rem(x + 3, NX), lax.rem(x + 1, NX), lax.rem(x + 2, NX)
    ym, yp, y2 = lax.rem(y + 3, NY), lax.rem(y + 1, NY), lax.rem(y + 2, NY)

    def chip(cx, cy, cc):
        return (z, (cx * NY + cy) * NC + cc)

    odd = lax.rem(z, 2)

    def columns(j, size):
        first = QKV_CHUNKS if j >= QKV_CHUNKS else 0
        if j in PAIRS:
            return pl.multiple_of((j - first + odd) * size, size)
        if j in PAIRS.values():
            return pl.multiple_of((j - first - odd) * size, size)
        return (j - first) * size

    at_xp, at_xm, at_yp, at_ym = chip(xp, y, c), chip(xm, y, c), chip(x, yp, c), chip(x, ym, c)
    at_x2, at_y2 = chip(x2, y, c), chip(x, y2, c)
    sib = chip(x, y, 1 - c)
    low, high = (z, lax.rem(p + BANDS - 1, BANDS)), (z, lax.rem(p + 1, BANDS))

    def other(k):
        return lax.rem(z + (k + MEMBERS), MEMBERS)

    barrier = pltpu.get_barrier_semaphore()
    partners = [at_xp, at_xm, at_yp, at_ym, at_x2, at_y2, sib, low, high]
    partners += [(other(k), p) for k in range(-REACH, REACH + 1) if k]
    for target in partners:
        pl.semaphore_signal(barrier, inc=1, device_id=target, device_id_type=MESH)

    loads = []

    def load(src, dst):
        copy = pltpu.make_async_copy(src, dst, in_sem.at[len(loads)])
        copy.start()
        loads.append(copy)

    gathered = [j for j in range(CHUNKS) if j not in PAIRS.values()]
    for j in gathered:
        if j < QKV_CHUNKS:
            for part in range(3):
                load(
                    wqkv_hbm.at[:, pl.ds(part * D + columns(j, COLS), COLS)],
                    wq.at[j, x, y, c, :, pl.ds(part * COLS, COLS)],
                )
        else:
            load(wout_hbm.at[:, pl.ds(columns(j, OUT_COLS), OUT_COLS)], wo.at[j - QKV_CHUNKS, x, y, c])
    weight_loads = len(loads)
    small = ((truth_hbm, truth_ref), (gain_hbm, gain_ref), (edge_hbm, edge_ref), (dec_hbm, dec_ref))
    for src, dst in ((tok_hbm, tok_ref),) + small:
        load(src, dst)
    for copy in loads[: weight_loads + 2]:
        copy.wait()
    cells = jnp.concatenate([truth_ref[0], truth_ref[1], jnp.zeros((8, V), BF16)], axis=0)
    truths[z] = jnp.concatenate([cells, jnp.zeros((16, TOK - V), BF16)], axis=1)
    pl.semaphore_wait(barrier, len(partners))

    sent = []

    def send(src, dst, ssem, rsem, target):
        copy = pltpu.make_async_remote_copy(
            src_ref=src, dst_ref=dst, send_sem=ssem, recv_sem=rsem, device_id=target, device_id_type=MESH
        )
        copy.start()
        sent.append(copy)

    def arrive(dst, ssem, rsem):
        pltpu.make_async_remote_copy(
            src_ref=dst, dst_ref=dst, send_sem=ssem, recv_sem=rsem, device_id=sib, device_id_type=MESH
        ).wait_recv()

    def buf(j):
        return (wq.at[j], 3 * COLS) if j < QKV_CHUNKS else (wo.at[j - QKV_CHUNKS], OUT_COLS)

    A, B = pl.ds(0, 16), pl.ds(16, 16)
    ALL = slice(None)

    def pieces(j, step):
        _, n = buf(j)
        lo, hi = pl.ds(0, n // 2), pl.ds(n // 2, n // 2)
        if step == "start":
            near = [
                (0, (x, y, c, A), at_xp, (xm, y, c, A)),
                (1, (x, y, c, A), at_xm, (xp, y, c, A)),
                (2, (x, y, c, B), at_yp, (x, ym, c, B)),
                (3, (x, y, c, B), at_ym, (x, yp, c, B)),
            ]
            far = [(4, (x, y, c, A), at_x2, (x2, y, c, A)), (6, (x, y, c, B), at_y2, (x, y2, c, B))]
            return near + far if j in FAR_FIRST else near
        if step == "relay":
            return [
                (4, (xm, y, c, A, lo), at_xp, (x2, y, c, A, lo)),
                (5, (xp, y, c, A, hi), at_xm, (x2, y, c, A, hi)),
                (6, (x, ym, c, B, lo), at_yp, (x, y2, c, B, lo)),
                (7, (x, yp, c, B, hi), at_ym, (x, y2, c, B, hi)),
            ]
        if step == "second":
            near = [
                (8, (ALL, y, c, A), at_yp, (ALL, ym, c, A)),
                (9, (ALL, y, c, A), at_ym, (ALL, yp, c, A)),
                (10, (x, ALL, c, B), at_xp, (xm, ALL, c, B)),
                (11, (x, ALL, c, B), at_xm, (xp, ALL, c, B)),
            ]
            far = [(12, (ALL, y, c, A), at_y2, (ALL, y2, c, A)), (14, (x, ALL, c, B), at_x2, (x2, ALL, c, B))]
            return far + near if j in FAR_SECOND else near
        if step == "again":
            return [
                (12, (ALL, ym, c, A, lo), at_yp, (ALL, y2, c, A, lo)),
                (13, (ALL, yp, c, A, hi), at_ym, (ALL, y2, c, A, hi)),
                (14, (xm, ALL, c, B, lo), at_xp, (x2, ALL, c, B, lo)),
                (15, (xp, ALL, c, B, hi), at_xm, (x2, ALL, c, B, hi)),
            ]
        if step == "core_near":
            return [(16, (ALL, y, c, A), sib, (ALL, y, 1 - c, A)), (17, (x, ALL, c, B), sib, (x, ALL, 1 - c, B))]
        if step == "core_next":
            return [
                (18, (ALL, ym, c, A), sib, (ALL, ym, 1 - c, A)),
                (19, (ALL, yp, c, A), sib, (ALL, yp, 1 - c, A)),
                (20, (xm, ALL, c, B), sib, (xm, ALL, 1 - c, B)),
                (21, (xp, ALL, c, B), sib, (xp, ALL, 1 - c, B)),
            ]
        return [(22, (ALL, y2, c, A), sib, (ALL, y2, 1 - c, A)), (23, (x2, ALL, c, B), sib, (x2, ALL, 1 - c, B))]

    def go(j, step):
        ref, _ = buf(j)
        for i, src, target, _ in pieces(j, step):
            send(ref.at[src], ref.at[src], w_ssem.at[j, i], w_rsem.at[j, i], target)

    def got(j, *steps):
        ref, _ = buf(j)
        for step in steps:
            for i, _, _, dst in pieces(j, step):
                arrive(ref.at[dst], w_ssem.at[j, i], w_rsem.at[j, i])

    up, down = (other(1), p), (other(-1), p)
    Z_NEAR = [
        (24, (ALL, ym, c, A), up), (25, (ALL, y, c, A), up), (26, (ALL, yp, c, A), up),
        (27, (xm, ALL, c, B), down), (28, (x, ALL, c, B), down), (29, (xp, ALL, c, B), down),
    ]
    Z_LAST = [(30, (ALL, y2, c, A), up), (31, (x2, ALL, c, B), down)]

    def go_z(j, part):
        if j in PAIRS:
            mine, theirs, k = buf(j)[0], buf(PAIRS[j])[0], PAIRS[j]
            for i, where, target in part:
                send(mine.at[where], theirs.at[where], w_ssem.at[k, i], w_rsem.at[k, i], target)

    def reach(ref, ssem, rsem):
        for d in range(REACH, 0, -1):
            send(ref.at[z], ref.at[z], ssem.at[d], rsem.at[d], (other(d), p))
            send(ref.at[z], ref.at[z], ssem.at[REACH + d], rsem.at[REACH + d], (other(-d), p))

    def relay(ref, ssem, rsem):
        behind, ahead = ref.at[other(-REACH)], ref.at[other(REACH)]
        arrive(behind, ssem.at[REACH], rsem.at[REACH])
        arrive(ahead, ssem.at[2 * REACH], rsem.at[2 * REACH])
        rows = ref.shape[1] // 2
        if rows % 16 == 0:
            first, second = pl.ds(0, rows), pl.ds(rows, rows)
            send(behind.at[first], behind.at[first], ssem.at[12], rsem.at[12], (other(REACH), p))
            send(ahead.at[second], ahead.at[second], ssem.at[16], rsem.at[16], (other(-REACH), p))
        else:
            send(behind, behind, ssem.at[12], rsem.at[12], (other(REACH), p))
        for d in range(REACH - 1, 0, -1):
            send(behind, behind, ssem.at[8 + d], rsem.at[8 + d], (other(d), p))
            send(ahead, ahead, ssem.at[12 + d], rsem.at[12 + d], (other(-d), p))

    def reached_near(ref, ssem, rsem):
        for d in range(1, REACH):
            arrive(ref.at[other(-d)], ssem.at[d], rsem.at[d])
            arrive(ref.at[other(d)], ssem.at[REACH + d], rsem.at[REACH + d])

    def reached_far(ref, ssem, rsem):
        for d in range(1, REACH):
            arrive(ref.at[other(-REACH - d)], ssem.at[8 + d], rsem.at[8 + d])
            arrive(ref.at[other(REACH + d)], ssem.at[12 + d], rsem.at[12 + d])
        opposite = ref.at[other(MEMBERS // 2)]
        rows = ref.shape[1] // 2
        if rows % 16 == 0:
            arrive(opposite.at[pl.ds(0, rows)], ssem.at[12], rsem.at[12])
            arrive(opposite.at[pl.ds(rows, rows)], ssem.at[16], rsem.at[16])
        else:
            arrive(opposite, ssem.at[12], rsem.at[12])

    go(0, "start")
    for j in gathered[1:]:
        go(j, "start")
    reach(truths, t_ssem, t_rsem)

    def norm(rows):
        return (rms_scale(rows[...].astype(F32)) * gain_ref[...]).astype(BF16)

    for copy in loads[weight_loads + 2 :]:
        copy.wait()
    normed[TOK : 2 * TOK] = norm(tok_ref)
    local = jnp.concatenate([edge_ref[0], edge_ref[1]], axis=1) - (p - 1) * TOK
    nodes = iota((WIN, TOK), 0)
    total = jnp.zeros((WIN, TOK), F32)
    for k in range(FAN):
        total += jnp.where(local[k : k + 1] == nodes, 1.0, 0.0)
    count[...] = total.T
    dec[...] = jnp.zeros_like(dec)
    dec[:V] = dec_ref[...]
    row, col = iota((MEMBERS * TOK, TILE), 0), iota((MEMBERS * TOK, TILE), 1)
    cell = ((col >> 3) & 1) * 64 + ((4 * z - 2 + (col & 7)) & 63)
    pick[...] = hot(row == (col >> 4) * TOK + cell)

    def heads(j):
        weight = wq[j].reshape(D, 3 * COLS)
        query = dot(normed[TOK : 2 * TOK], weight[:, :COLS]).astype(BF16)
        keyval = dot(normed[...], weight[:, COLS:]).astype(BF16)
        key, value = keyval[:, :COLS], keyval[:, COLS:]
        head_of = iota((TOK, COLS), 1) >> 6
        spread = jnp.concatenate(
            [jnp.where(head_of == h, query, jnp.zeros_like(query)) for h in range(HEADS_C)], axis=0
        )
        scores = dot_t(spread, key) * 0.125
        times = count[...]
        probs = []
        for h in range(HEADS_C):
            s = jnp.where(times > 0.0, scores[h * TOK : (h + 1) * TOK], -1e30)
            expo = jnp.exp(s - jnp.max(s, axis=-1, keepdims=True)) * times
            probs.append((expo * (1.0 / jnp.sum(expo, axis=-1, keepdims=True))).astype(BF16))
        mixed = dot(jnp.concatenate(probs, axis=0), value)
        out = jnp.zeros((TOK, COLS), F32)
        for h in range(HEADS_C):
            out = jnp.where(head_of == h, mixed[h * TOK : (h + 1) * TOK], out)
        att[:, pl.ds(columns(j, COLS), COLS)] = out.astype(BF16)

    def project(j):
        i = j - QKV_CHUNKS
        where = pl.ds(columns(j, OUT_COLS), OUT_COLS)
        state[:, where] = tok_ref[:, where].astype(F32) + dot(att[...], wo[i].reshape(D, OUT_COLS))

    for step, j in ORDER:
        if step == "halo":
            send(tok_ref, halo.at[1], h_ssem.at[1], h_rsem.at[1], low)
            send(tok_ref, halo.at[0], h_ssem.at[0], h_rsem.at[0], high)
            continue
        if step == "truth":
            relay(truths, t_ssem, t_rsem)
            continue
        if step == "first":
            got(j, "start")
            go(j, "second")
            go(j, "core_near")
        elif step == "relay":
            got(j, "start")
            go(j, "relay")
        elif step == "second":
            got(j, "relay")
            go(j, "second")
            go(j, "core_near")
        elif step == "again":
            got(j, "second")
            go_z(j, Z_NEAR)
            go(j, "again")
            go(j, "core_next")
        elif step == "core" and j in PAIRS.values():
            ref = buf(j)[0]
            for i, where, _ in Z_NEAR + Z_LAST:
                arrive(ref.at[where], w_ssem.at[j, i], w_rsem.at[j, i])
            send(ref.at[ALL, ALL, c], ref.at[ALL, ALL, c], w_ssem.at[j, 32], w_rsem.at[j, 32], sib)
        elif step == "core":
            if j in FAR_SECOND:
                got(j, "second")
                go(j, "core_next")
            else:
                got(j, "again")
            go_z(j, Z_LAST)
            go(j, "core_last")
        elif step == "done" and j in PAIRS.values():
            arrive(buf(j)[0].at[ALL, ALL, 1 - c], w_ssem.at[j, 32], w_rsem.at[j, 32])
        elif step == "done":
            got(j, "core_near", "core_next", "core_last")
        elif step == "out":
            project(j)
        elif step == "heads":
            if j == 0:
                arrive(halo.at[0], h_ssem.at[0], h_rsem.at[0])
                arrive(halo.at[1], h_ssem.at[1], h_rsem.at[1])
                normed[:TOK] = norm(halo.at[0])
                normed[2 * TOK :] = norm(halo.at[1])
            heads(j)

    fields[z] = dot_t(dec[...], rms_scale(state[...]).astype(BF16)).astype(BF16)
    before = len(sent)
    reach(fields, f_ssem, f_rsem)
    for copy in sent[:before]:
        copy.wait_send()

    reached_near(truths, t_ssem, t_rsem)
    reached_far(truths, t_ssem, t_rsem)
    row, col = iota((TOK, TILE), 0), iota((TOK, TILE), 1)
    source = ((row & 63) >> 2) * 16 + (row >> 6) * 4 + (row & 3)
    truth_rows = dot(hot(col == source), truths[...].reshape(TILE, TOK)).astype(BF16)
    eye = hot(iota((VP, TOK), 0) == iota((VP, TOK), 1))
    truth_b = dot_t(eye, truth_rows)
    spot = ((col >> 3) & 1) * 64 + ((4 * z - 2 + (col & 7)) & 63)
    truth_tile = dot(truth_b.astype(BF16), hot(row == spot))
    own = fields[z].astype(F32)

    def row_sum(grid):
        return jnp.sum(grid * grid, axis=0, keepdims=True)

    def own_row(k):
        e_all[1, k : k + 1, :TOK] = row_sum(own - fields[other(k)].astype(F32))

    e_all[1, 0:1, :TOK] = row_sum(own - truth_b)
    e_all[1, 8:16, TOK:] = jnp.zeros((8, TILE), F32)
    relay(fields, f_ssem, f_rsem)
    reached_near(fields, f_ssem, f_rsem)
    for k in range(1, REACH + 1):
        own_row(k)
        own_row(MEMBERS - k)
    reached_far(fields, f_ssem, f_rsem)
    for k in range(REACH + 1, MEMBERS - REACH):
        own_row(k)
    tile = dot(jnp.concatenate([fields[m] for m in range(MEMBERS)], axis=1), pick[...])
    e_all[1, 0:1, TOK:] = row_sum(tile - truth_tile)
    for k in range(1, MEMBERS // 2 + 1):
        e_all[1, k : k + 1, TOK:] = row_sum(tile - pltpu.roll(tile, TILE - 16 * k, axis=1))

    send(e_all.at[1], e_all.at[0], e_ssem.at[0], e_rsem.at[0], high)
    send(e_all.at[1], e_all.at[2], e_ssem.at[1], e_rsem.at[1], low)
    arrive(e_all.at[0], e_ssem.at[0], e_rsem.at[0])
    arrive(e_all.at[2], e_ssem.at[1], e_rsem.at[1])

    below = jnp.where(p > 0, 1.0, 0.0)
    above = jnp.where(p < BANDS - 1, 1.0, 0.0)
    e_low, e_own, e_high = e_all[0] * below, e_all[1], e_all[2] * above

    lane = iota((MEMBERS, TOK), 1)
    north, lon = lane < 64, lane & 63

    def swap(grid):
        return pltpu.roll(grid, 64, axis=1)

    def along(grid):
        west = jnp.where(lon == 0, pltpu.roll(grid, 65, axis=1), pltpu.roll(grid, 1, axis=1))
        east = jnp.where(lon == 63, pltpu.roll(grid, 63, axis=1), pltpu.roll(grid, TOK - 1, axis=1))
        return west + grid + east

    r_low, r_own, r_high = e_low[:, :TOK], e_own[:, :TOK], e_high[:, :TOK]
    s_low, s_own, s_high = swap(r_low), swap(r_own), swap(r_high)
    box_own = along(r_own + s_own + jnp.where(north, s_low, s_high))
    box_out = along(s_own + jnp.where(north, r_high + s_high, r_low + s_low))
    scale = jnp.where(iota((MEMBERS, TOK), 0) == 0, 1.0, 1.0 / (MEMBERS - 1))
    c_own = scale / jnp.sqrt(box_own / PATCH + EPS)
    c_out = scale / jnp.sqrt(box_out / PATCH + EPS) * jnp.where(north, above, below)
    btot = along(c_own + swap(c_own) + swap(c_out))
    grad = btot[0:1] * (own - truth_b)
    for k in range(1, MEMBERS):
        grad = grad - btot[k : k + 1] * (own - fields[other(k)].astype(F32))
    grad_ref[...] = grad[:V]

    lane = iota((MEMBERS, TILE), 1)
    north = ((lane >> 3) & 1) == 0

    def swap_tile(grid):
        return jnp.where(north, pltpu.roll(grid, TILE - 8, axis=1), pltpu.roll(grid, 8, axis=1))

    t_own = e_own[:, TOK:]
    rows = t_own + swap_tile(t_own) + jnp.where(north, swap_tile(e_low[:, TOK:]), swap_tile(e_high[:, TOK:]))
    box = pltpu.roll(rows, 1, axis=1) + rows + pltpu.roll(rows, TILE - 1, axis=1)
    apart = iota((MEMBERS, TILE), 0)
    pair = 0.5 / (MEMBERS * (MEMBERS - 1))
    weight = jnp.where(apart == 0, 1.0 / MEMBERS, jnp.where(apart < MEMBERS // 2, -2.0 * pair, -pair))
    weight = jnp.where(apart > MEMBERS // 2, 0.0, weight)
    part = jnp.sum(jnp.sqrt(box / PATCH + EPS) * weight, axis=0, keepdims=True)
    for shift in (128, 64, 32, 16):
        part = part + pltpu.roll(part, shift, axis=1)
    score_ref[0:1] = part[:, 2:6]
    score_ref[1:2] = part[:, 10:14]
    for copy in sent[before:]:
        copy.wait_send()


def on_device(tokens, norm_gain, qkv_weight, out_weight, decode_weight, edges, truth):
    vmem = pl.BlockSpec(memory_space=pltpu.VMEM)
    dma = pltpu.SemaphoreType.DMA
    score, grad = pl.pallas_call(
        kernel,
        out_shape=(jax.ShapeDtypeStruct((2, 4), F32), jax.ShapeDtypeStruct((V, TOK), F32)),
        in_specs=[pl.BlockSpec(memory_space=pltpu.HBM)] * 7,
        out_specs=(vmem, vmem),
        scratch_shapes=[
            pltpu.VMEM((TOK, D), BF16),
            pltpu.VMEM((1, D), F32),
            pltpu.VMEM((V, D), BF16),
            pltpu.VMEM((2, FAN, 64), jnp.int32),
            pltpu.VMEM((2, 4, V), BF16),
            pltpu.VMEM((QKV_CHUNKS, NX, NY, NC, 32, 3 * COLS), BF16),
            pltpu.VMEM((OUT_CHUNKS, NX, NY, NC, 32, OUT_COLS), BF16),
            pltpu.VMEM((2, TOK, D), BF16),
            pltpu.VMEM((WIN, D), BF16),
            pltpu.VMEM((TOK, WIN), F32),
            pltpu.VMEM((TOK, D), BF16),
            pltpu.VMEM((TOK, D), F32),
            pltpu.VMEM((VP, D), BF16),
            pltpu.VMEM((MEMBERS, 16, TOK), BF16),
            pltpu.VMEM((MEMBERS, VP, TOK), BF16),
            pltpu.VMEM((MEMBERS * TOK, TILE), BF16),
            pltpu.VMEM((3, MEMBERS, TOK + TILE), F32),
            dma((3 * QKV_CHUNKS + OUT_CHUNKS + 5,)),
            dma((CHUNKS, STEPS)),
            dma((CHUNKS, STEPS)),
            dma((2,)),
            dma((2,)),
            dma((4 * REACH + 1,)),
            dma((4 * REACH + 1,)),
            dma((4 * REACH + 1,)),
            dma((4 * REACH + 1,)),
            dma((2,)),
            dma((2,)),
        ],
        compiler_params=pltpu.CompilerParams(
            collective_id=0, has_side_effects=True, vmem_limit_bytes=48 * 1024 * 1024
        ),
    )(
        *(pltpu.with_memory_space_constraint(a, pltpu.HBM) for a in (
            tokens.reshape(TOK, D),
            norm_gain.reshape(1, D),
            qkv_weight,
            out_weight,
            decode_weight.T,
            edges.transpose(0, 2, 1),
            truth.transpose(1, 2, 0),
        ))
    )
    return score, grad.reshape(1, V, 2, 64)


def solution(mesh):
    in_specs = (
        P("member", "mp", None, None),
        P(),
        P("mp", None),
        P("mp", None),
        P(),
        P("mp", None, None),
        P(None, "mp", "member"),
    )
    out_specs = (P("mp", "member"), P("member", None, "mp", None))
    return jax.shard_map(on_device, mesh=mesh, in_specs=in_specs, out_specs=out_specs, check_vma=False)
```

```python
import jax
import jax.numpy as jnp
from jax import lax
from jax.experimental import pallas as pl
from jax.experimental.pallas import tpu as pltpu
from jax.sharding import PartitionSpec as P

MESH = pl.DeviceIdType.MESH
F32, BF16 = jnp.float32, jnp.bfloat16
EPS = 1e-05
NX, NY, NC = 4, 4, 2
MEMBERS = 16
BANDS = NX * NY * NC
TOK = 128
WIN = 3 * TOK
D = 1024
V = 90
VP = 96
FAN = 16
HEADS_C = 4
QKV_CHUNKS = 4
OUT_CHUNKS = 2
CHUNKS = QKV_CHUNKS + OUT_CHUNKS
COLS = 256
OUT_COLS = D // OUT_CHUNKS
STEPS = 33
REACH = 4
HALF = VP // 2
TILE = MEMBERS * 16
PATCH = 9.0 * V
FAR_FIRST, FAR_SECOND = (0, 2, 3), (CHUNKS - 1,)
PAIRS = {0: 1}
ORDER = (
    ("first", 0), ("greet", 2), ("first", 2), ("first", 3), ("greet", 3), ("relay", 4), ("relay", 5), ("again", 0), ("halo", 0), ("again", 2),
    ("core", 0), ("greet", 4), ("second", 4), ("again", 3), ("second", 5), ("core", 2), ("truth", 0), ("done", 0), ("heads", 0),
    ("core", 1), ("again", 4), ("core", 3), ("done", 2), ("heads", 2), ("done", 1), ("heads", 1), ("core", 4),
    ("core", 5), ("done", 3), ("heads", 3), ("done", 4), ("out", 4), ("done", 5), ("out", 5),
)


def iota(shape, dim):
    return lax.broadcasted_iota(jnp.int32, shape, dim)


def hot(mask, dtype=BF16):
    return jnp.where(mask, 1.0, 0.0).astype(dtype)


def dot(a, b, **kw):
    return jnp.dot(a, b, preferred_element_type=F32, **kw)


def dot_t(a, b, **kw):
    return lax.dot_general(a, b, (((1,), (1,)), ((), ())), preferred_element_type=F32, **kw)


def rms_scale(v):
    return v * lax.rsqrt(jnp.mean(v * v, axis=-1, keepdims=True) + EPS)


def kernel(
    tok_hbm, gain_hbm, wqkv_hbm, wout_hbm, dec_hbm, edge_hbm, truth_hbm,
    score_ref, grad_ref,
    tok_ref, gain_ref, dec_ref, edge_ref, truth_ref, wq, wo, halo, normed, count, att, state, dec, truths, fields, pick, e_all,
    in_sem, w_ssem, w_rsem, h_ssem, h_rsem, t_ssem, t_rsem, f_ssem, f_rsem, e_ssem, e_rsem, near_sem,
):
    z = lax.axis_index("member")
    p = lax.axis_index("mp")
    x, y, c = lax.div(p, NY * NC), lax.rem(lax.div(p, NC), NY), lax.rem(p, NC)
    xm, xp, x2 = lax.rem(x + 3, NX), lax.rem(x + 1, NX), lax.rem(x + 2, NX)
    ym, yp, y2 = lax.rem(y + 3, NY), lax.rem(y + 1, NY), lax.rem(y + 2, NY)

    def chip(cx, cy, cc):
        return (z, (cx * NY + cy) * NC + cc)

    odd = lax.rem(z, 2)

    def columns(j, size):
        first = QKV_CHUNKS if j >= QKV_CHUNKS else 0
        if j in PAIRS:
            return pl.multiple_of((j - first + odd) * size, size)
        if j in PAIRS.values():
            return pl.multiple_of((j - first - odd) * size, size)
        return (j - first) * size

    at_xp, at_xm, at_yp, at_ym = chip(xp, y, c), chip(xm, y, c), chip(x, yp, c), chip(x, ym, c)
    at_x2, at_y2 = chip(x2, y, c), chip(x, y2, c)
    sib = chip(x, y, 1 - c)
    low, high = (z, lax.rem(p + BANDS - 1, BANDS)), (z, lax.rem(p + 1, BANDS))

    def other(k):
        return lax.rem(z + (k + MEMBERS), MEMBERS)

    barrier = pltpu.get_barrier_semaphore()
    partners = [at_xp, at_xm, at_yp, at_ym, at_x2, at_y2, sib, low, high]
    partners += [(other(k), p) for k in (-1, 1)]
    for target in partners:
        pl.semaphore_signal(barrier, inc=1, device_id=target, device_id_type=MESH)

    loads = []

    def load(src, dst):
        copy = pltpu.make_async_copy(src, dst, in_sem.at[len(loads)])
        copy.start()
        loads.append(copy)

    gathered = [j for j in range(CHUNKS) if j not in PAIRS.values()]
    for j in gathered:
        if j < QKV_CHUNKS:
            for part in range(3):
                load(
                    wqkv_hbm.at[:, pl.ds(part * D + columns(j, COLS), COLS)],
                    wq.at[j, x, y, c, :, pl.ds(part * COLS, COLS)],
                )
        else:
            load(wout_hbm.at[:, pl.ds(columns(j, OUT_COLS), OUT_COLS)], wo.at[j - QKV_CHUNKS, x, y, c])
    weight_loads = len(loads)
    small = ((truth_hbm, truth_ref), (gain_hbm, gain_ref), (edge_hbm, edge_ref), (dec_hbm, dec_ref))
    for src, dst in ((tok_hbm, tok_ref),) + small:
        load(src, dst)
    for copy in loads[: weight_loads + 2]:
        copy.wait()
    cells = jnp.concatenate([truth_ref[0], truth_ref[1], jnp.zeros((8, V), BF16)], axis=0)
    truths[z] = jnp.concatenate([cells, jnp.zeros((16, TOK - V), BF16)], axis=1)
    pl.semaphore_wait(barrier, len(partners))

    sent = []

    def send(src, dst, ssem, rsem, target):
        copy = pltpu.make_async_remote_copy(
            src_ref=src, dst_ref=dst, send_sem=ssem, recv_sem=rsem, device_id=target, device_id_type=MESH
        )
        copy.start()
        sent.append(copy)

    def arrive(dst, ssem, rsem):
        pltpu.make_async_remote_copy(
            src_ref=dst, dst_ref=dst, send_sem=ssem, recv_sem=rsem, device_id=sib, device_id_type=MESH
        ).wait_recv()

    def buf(j):
        return (wq.at[j], 3 * COLS) if j < QKV_CHUNKS else (wo.at[j - QKV_CHUNKS], OUT_COLS)

    A, B = pl.ds(0, 16), pl.ds(16, 16)
    ALL = slice(None)

    def pieces(j, step):
        _, n = buf(j)
        lo, hi = pl.ds(0, n // 2), pl.ds(n // 2, n // 2)
        if step == "start":
            near = [
                (0, (x, y, c, A), at_xp, (xm, y, c, A)),
                (1, (x, y, c, A), at_xm, (xp, y, c, A)),
                (2, (x, y, c, B), at_yp, (x, ym, c, B)),
                (3, (x, y, c, B), at_ym, (x, yp, c, B)),
            ]
            far = [(4, (x, y, c, A), at_x2, (x2, y, c, A)), (6, (x, y, c, B), at_y2, (x, y2, c, B))]
            return near + far if j in FAR_FIRST else near
        if step == "relay":
            return [
                (4, (xm, y, c, A, lo), at_xp, (x2, y, c, A, lo)),
                (5, (xp, y, c, A, hi), at_xm, (x2, y, c, A, hi)),
                (6, (x, ym, c, B, lo), at_yp, (x, y2, c, B, lo)),
                (7, (x, yp, c, B, hi), at_ym, (x, y2, c, B, hi)),
            ]
        if step == "second":
            near = [
                (8, (ALL, y, c, A), at_yp, (ALL, ym, c, A)),
                (9, (ALL, y, c, A), at_ym, (ALL, yp, c, A)),
                (10, (x, ALL, c, B), at_xp, (xm, ALL, c, B)),
                (11, (x, ALL, c, B), at_xm, (xp, ALL, c, B)),
            ]
            far = [(12, (ALL, y, c, A), at_y2, (ALL, y2, c, A)), (14, (x, ALL, c, B), at_x2, (x2, ALL, c, B))]
            return far + near if j in FAR_SECOND else near
        if step == "again":
            return [
                (12, (ALL, ym, c, A, lo), at_yp, (ALL, y2, c, A, lo)),
                (13, (ALL, yp, c, A, hi), at_ym, (ALL, y2, c, A, hi)),
                (14, (xm, ALL, c, B, lo), at_xp, (x2, ALL, c, B, lo)),
                (15, (xp, ALL, c, B, hi), at_xm, (x2, ALL, c, B, hi)),
            ]
        if step == "core_near":
            return [(16, (ALL, y, c, A), sib, (ALL, y, 1 - c, A)), (17, (x, ALL, c, B), sib, (x, ALL, 1 - c, B))]
        if step == "core_next":
            return [
                (18, (ALL, ym, c, A), sib, (ALL, ym, 1 - c, A)),
                (19, (ALL, yp, c, A), sib, (ALL, yp, 1 - c, A)),
                (20, (xm, ALL, c, B), sib, (xm, ALL, 1 - c, B)),
                (21, (xp, ALL, c, B), sib, (xp, ALL, 1 - c, B)),
            ]
        return [(22, (ALL, y2, c, A), sib, (ALL, y2, 1 - c, A)), (23, (x2, ALL, c, B), sib, (x2, ALL, 1 - c, B))]

    def go(j, step):
        ref, _ = buf(j)
        for i, src, target, _ in pieces(j, step):
            send(ref.at[src], ref.at[src], w_ssem.at[j, i], w_rsem.at[j, i], target)

    def got(j, *steps):
        ref, _ = buf(j)
        for step in steps:
            for i, _, _, dst in pieces(j, step):
                arrive(ref.at[dst], w_ssem.at[j, i], w_rsem.at[j, i])

    up, down = (other(1), p), (other(-1), p)
    Z_NEAR = [
        (24, (ALL, ym, c, A), up), (25, (ALL, y, c, A), up), (26, (ALL, yp, c, A), up),
        (27, (xm, ALL, c, B), down), (28, (x, ALL, c, B), down), (29, (xp, ALL, c, B), down),
    ]
    Z_LAST = [(30, (ALL, y2, c, A), up), (31, (x2, ALL, c, B), down)]

    def go_z(j, part):
        if j in PAIRS:
            mine, theirs, k = buf(j)[0], buf(PAIRS[j])[0], PAIRS[j]
            for i, where, target in part:
                send(mine.at[where], theirs.at[where], w_ssem.at[k, i], w_rsem.at[k, i], target)

    def reach(ref, ssem, rsem):
        for d in range(REACH, 0, -1):
            send(ref.at[z], ref.at[z], ssem.at[d], rsem.at[d], (other(d), p))
            send(ref.at[z], ref.at[z], ssem.at[REACH + d], rsem.at[REACH + d], (other(-d), p))

    def relay(ref, ssem, rsem):
        behind, ahead = ref.at[other(-REACH)], ref.at[other(REACH)]
        arrive(behind, ssem.at[REACH], rsem.at[REACH])
        arrive(ahead, ssem.at[2 * REACH], rsem.at[2 * REACH])
        rows = ref.shape[1] // 2
        if rows % 16 == 0:
            first, second = pl.ds(0, rows), pl.ds(rows, rows)
            send(behind.at[first], behind.at[first], ssem.at[12], rsem.at[12], (other(REACH), p))
            send(ahead.at[second], ahead.at[second], ssem.at[16], rsem.at[16], (other(-REACH), p))
        else:
            send(behind, behind, ssem.at[12], rsem.at[12], (other(REACH), p))
        for d in range(REACH - 1, 0, -1):
            send(behind, behind, ssem.at[8 + d], rsem.at[8 + d], (other(d), p))
            send(ahead, ahead, ssem.at[12 + d], rsem.at[12 + d], (other(-d), p))

    def reached_near(ref, ssem, rsem):
        for d in range(1, REACH):
            arrive(ref.at[other(-d)], ssem.at[d], rsem.at[d])
            arrive(ref.at[other(d)], ssem.at[REACH + d], rsem.at[REACH + d])

    def reached_far(ref, ssem, rsem):
        for d in range(1, REACH):
            arrive(ref.at[other(-REACH - d)], ssem.at[8 + d], rsem.at[8 + d])
            arrive(ref.at[other(REACH + d)], ssem.at[12 + d], rsem.at[12 + d])
        opposite = ref.at[other(MEMBERS // 2)]
        rows = ref.shape[1] // 2
        if rows % 16 == 0:
            arrive(opposite.at[pl.ds(0, rows)], ssem.at[12], rsem.at[12])
            arrive(opposite.at[pl.ds(rows, rows)], ssem.at[16], rsem.at[16])
        else:
            arrive(opposite, ssem.at[12], rsem.at[12])

    def greet(n):
        if n > 1:
            pl.semaphore_wait(near_sem.at[n - 2, 0], 1)
            pl.semaphore_wait(near_sem.at[n - 2, 1], 1)
        if n < REACH:
            pl.semaphore_signal(near_sem.at[n - 1, 0], inc=1, device_id=up, device_id_type=MESH)
            pl.semaphore_signal(near_sem.at[n - 1, 1], inc=1, device_id=down, device_id_type=MESH)

    go(0, "start")
    for j in gathered[1:]:
        go(j, "start")
    greet(1)

    def norm(rows):
        return (rms_scale(rows[...].astype(F32)) * gain_ref[...]).astype(BF16)

    for copy in loads[weight_loads + 2 :]:
        copy.wait()
    normed[TOK : 2 * TOK] = norm(tok_ref)
    local = jnp.concatenate([edge_ref[0], edge_ref[1]], axis=1) - (p - 1) * TOK
    nodes = iota((WIN, TOK), 0)
    total = jnp.zeros((WIN, TOK), F32)
    for k in range(FAN):
        total += jnp.where(local[k : k + 1] == nodes, 1.0, 0.0)
    count[...] = total.T
    dec[...] = jnp.zeros_like(dec)
    dec[:V] = dec_ref[...]
    row, col = iota((MEMBERS * TOK, TILE), 0), iota((MEMBERS * TOK, TILE), 1)
    cell = ((col >> 3) & 1) * 64 + ((4 * z - 2 + (col & 7)) & 63)
    pick[...] = hot(row == (col >> 4) * TOK + cell)

    def heads(j):
        weight = wq[j].reshape(D, 3 * COLS)
        query = dot(normed[TOK : 2 * TOK], weight[:, :COLS]).astype(BF16)
        keyval = dot(normed[...], weight[:, COLS:]).astype(BF16)
        key, value = keyval[:, :COLS], keyval[:, COLS:]
        head_of = iota((TOK, COLS), 1) >> 6
        spread = jnp.concatenate(
            [jnp.where(head_of == h, query, jnp.zeros_like(query)) for h in range(HEADS_C)], axis=0
        )
        scores = dot_t(spread, key) * 0.125
        times = count[...]
        probs = []
        for h in range(HEADS_C):
            s = jnp.where(times > 0.0, scores[h * TOK : (h + 1) * TOK], -1e30)
            expo = jnp.exp(s - jnp.max(s, axis=-1, keepdims=True)) * times
            probs.append((expo * (1.0 / jnp.sum(expo, axis=-1, keepdims=True))).astype(BF16))
        mixed = dot(jnp.concatenate(probs, axis=0), value)
        out = jnp.zeros((TOK, COLS), F32)
        for h in range(HEADS_C):
            out = jnp.where(head_of == h, mixed[h * TOK : (h + 1) * TOK], out)
        att[:, pl.ds(columns(j, COLS), COLS)] = out.astype(BF16)

    def project(j):
        i = j - QKV_CHUNKS
        where = pl.ds(columns(j, OUT_COLS), OUT_COLS)
        state[:, where] = tok_ref[:, where].astype(F32) + dot(att[...], wo[i].reshape(D, OUT_COLS))

    for step, j in ORDER:
        if step == "halo":
            send(tok_ref, halo.at[1], h_ssem.at[1], h_rsem.at[1], low)
            send(tok_ref, halo.at[0], h_ssem.at[0], h_rsem.at[0], high)
            continue
        if step == "greet":
            greet(j)
            if j == REACH:
                reach(truths, t_ssem, t_rsem)
            continue
        if step == "truth":
            relay(truths, t_ssem, t_rsem)
            continue
        if step == "first":
            got(j, "start")
            go(j, "second")
            go(j, "core_near")
        elif step == "relay":
            got(j, "start")
            go(j, "relay")
        elif step == "second":
            got(j, "relay")
            go(j, "second")
            go(j, "core_near")
        elif step == "again":
            got(j, "second")
            go_z(j, Z_NEAR)
            go(j, "again")
            go(j, "core_next")
        elif step == "core" and j in PAIRS.values():
            ref = buf(j)[0]
            for i, where, _ in Z_NEAR + Z_LAST:
                arrive(ref.at[where], w_ssem.at[j, i], w_rsem.at[j, i])
            send(ref.at[ALL, ALL, c], ref.at[ALL, ALL, c], w_ssem.at[j, 32], w_rsem.at[j, 32], sib)
        elif step == "core":
            if j in FAR_SECOND:
                got(j, "second")
                go(j, "core_next")
            else:
                got(j, "again")
            go_z(j, Z_LAST)
            go(j, "core_last")
        elif step == "done" and j in PAIRS.values():
            arrive(buf(j)[0].at[ALL, ALL, 1 - c], w_ssem.at[j, 32], w_rsem.at[j, 32])
        elif step == "done":
            got(j, "core_near", "core_next", "core_last")
        elif step == "out":
            project(j)
        elif step == "heads":
            if j == 0:
                arrive(halo.at[0], h_ssem.at[0], h_rsem.at[0])
                arrive(halo.at[1], h_ssem.at[1], h_rsem.at[1])
                normed[:TOK] = norm(halo.at[0])
                normed[2 * TOK :] = norm(halo.at[1])
            heads(j)

    fields[z] = dot_t(dec[...], rms_scale(state[...]).astype(BF16)).astype(BF16)
    before = len(sent)
    reach(fields, f_ssem, f_rsem)
    for copy in sent[:before]:
        copy.wait_send()

    reached_near(truths, t_ssem, t_rsem)
    reached_far(truths, t_ssem, t_rsem)
    row, col = iota((TOK, TILE), 0), iota((TOK, TILE), 1)
    source = ((row & 63) >> 2) * 16 + (row >> 6) * 4 + (row & 3)
    truth_rows = dot(hot(col == source), truths[...].reshape(TILE, TOK)).astype(BF16)
    eye = hot(iota((VP, TOK), 0) == iota((VP, TOK), 1))
    truth_b = dot_t(eye, truth_rows)
    spot = ((col >> 3) & 1) * 64 + ((4 * z - 2 + (col & 7)) & 63)
    truth_tile = dot(truth_b.astype(BF16), hot(row == spot))
    own = fields[z].astype(F32)

    def row_sum(grid):
        return jnp.sum(grid * grid, axis=0, keepdims=True)

    def own_row(k):
        e_all[1, k : k + 1, :TOK] = row_sum(own - fields[other(k)].astype(F32))

    e_all[1, 0:1, :TOK] = row_sum(own - truth_b)
    e_all[1, 8:16, TOK:] = jnp.zeros((8, TILE), F32)
    relay(fields, f_ssem, f_rsem)
    reached_near(fields, f_ssem, f_rsem)
    for k in range(1, REACH + 1):
        own_row(k)
        own_row(MEMBERS - k)
    reached_far(fields, f_ssem, f_rsem)
    for k in range(REACH + 1, MEMBERS - REACH):
        own_row(k)
    tile = dot(jnp.concatenate([fields[m] for m in range(MEMBERS)], axis=1), pick[...])
    e_all[1, 0:1, TOK:] = row_sum(tile - truth_tile)
    for k in range(1, MEMBERS // 2 + 1):
        e_all[1, k : k + 1, TOK:] = row_sum(tile - pltpu.roll(tile, TILE - 16 * k, axis=1))

    send(e_all.at[1], e_all.at[0], e_ssem.at[0], e_rsem.at[0], high)
    send(e_all.at[1], e_all.at[2], e_ssem.at[1], e_rsem.at[1], low)
    arrive(e_all.at[0], e_ssem.at[0], e_rsem.at[0])
    arrive(e_all.at[2], e_ssem.at[1], e_rsem.at[1])

    below = jnp.where(p > 0, 1.0, 0.0)
    above = jnp.where(p < BANDS - 1, 1.0, 0.0)
    e_low, e_own, e_high = e_all[0] * below, e_all[1], e_all[2] * above

    lane = iota((MEMBERS, TOK), 1)
    north, lon = lane < 64, lane & 63

    def swap(grid):
        return pltpu.roll(grid, 64, axis=1)

    def along(grid):
        west = jnp.where(lon == 0, pltpu.roll(grid, 65, axis=1), pltpu.roll(grid, 1, axis=1))
        east = jnp.where(lon == 63, pltpu.roll(grid, 63, axis=1), pltpu.roll(grid, TOK - 1, axis=1))
        return west + grid + east

    r_low, r_own, r_high = e_low[:, :TOK], e_own[:, :TOK], e_high[:, :TOK]
    s_low, s_own, s_high = swap(r_low), swap(r_own), swap(r_high)
    box_own = along(r_own + s_own + jnp.where(north, s_low, s_high))
    box_out = along(s_own + jnp.where(north, r_high + s_high, r_low + s_low))
    scale = jnp.where(iota((MEMBERS, TOK), 0) == 0, 1.0, 1.0 / (MEMBERS - 1))
    c_own = scale / jnp.sqrt(box_own / PATCH + EPS)
    c_out = scale / jnp.sqrt(box_out / PATCH + EPS) * jnp.where(north, above, below)
    btot = along(c_own + swap(c_own) + swap(c_out))
    grad = btot[0:1] * (own - truth_b)
    for k in range(1, MEMBERS):
        grad = grad - btot[k : k + 1] * (own - fields[other(k)].astype(F32))
    grad_ref[...] = grad[:V]

    lane = iota((MEMBERS, TILE), 1)
    north = ((lane >> 3) & 1) == 0

    def swap_tile(grid):
        return jnp.where(north, pltpu.roll(grid, TILE - 8, axis=1), pltpu.roll(grid, 8, axis=1))

    t_own = e_own[:, TOK:]
    rows = t_own + swap_tile(t_own) + jnp.where(north, swap_tile(e_low[:, TOK:]), swap_tile(e_high[:, TOK:]))
    box = pltpu.roll(rows, 1, axis=1) + rows + pltpu.roll(rows, TILE - 1, axis=1)
    apart = iota((MEMBERS, TILE), 0)
    pair = 0.5 / (MEMBERS * (MEMBERS - 1))
    weight = jnp.where(apart == 0, 1.0 / MEMBERS, jnp.where(apart < MEMBERS // 2, -2.0 * pair, -pair))
    weight = jnp.where(apart > MEMBERS // 2, 0.0, weight)
    part = jnp.sum(jnp.sqrt(box / PATCH + EPS) * weight, axis=0, keepdims=True)
    for shift in (128, 64, 32, 16):
        part = part + pltpu.roll(part, shift, axis=1)
    score_ref[0:1] = part[:, 2:6]
    score_ref[1:2] = part[:, 10:14]
    for copy in sent[before:]:
        copy.wait_send()


def on_device(tokens, norm_gain, qkv_weight, out_weight, decode_weight, edges, truth):
    vmem = pl.BlockSpec(memory_space=pltpu.VMEM)
    dma = pltpu.SemaphoreType.DMA
    score, grad = pl.pallas_call(
        kernel,
        out_shape=(jax.ShapeDtypeStruct((2, 4), F32), jax.ShapeDtypeStruct((V, TOK), F32)),
        in_specs=[pl.BlockSpec(memory_space=pltpu.HBM)] * 7,
        out_specs=(vmem, vmem),
        scratch_shapes=[
            pltpu.VMEM((TOK, D), BF16),
            pltpu.VMEM((1, D), F32),
            pltpu.VMEM((V, D), BF16),
            pltpu.VMEM((2, FAN, 64), jnp.int32),
            pltpu.VMEM((2, 4, V), BF16),
            pltpu.VMEM((QKV_CHUNKS, NX, NY, NC, 32, 3 * COLS), BF16),
            pltpu.VMEM((OUT_CHUNKS, NX, NY, NC, 32, OUT_COLS), BF16),
            pltpu.VMEM((2, TOK, D), BF16),
            pltpu.VMEM((WIN, D), BF16),
            pltpu.VMEM((TOK, WIN), F32),
            pltpu.VMEM((TOK, D), BF16),
            pltpu.VMEM((TOK, D), F32),
            pltpu.VMEM((VP, D), BF16),
            pltpu.VMEM((MEMBERS, 16, TOK), BF16),
            pltpu.VMEM((MEMBERS, VP, TOK), BF16),
            pltpu.VMEM((MEMBERS * TOK, TILE), BF16),
            pltpu.VMEM((3, MEMBERS, TOK + TILE), F32),
            dma((3 * QKV_CHUNKS + OUT_CHUNKS + 5,)),
            dma((CHUNKS, STEPS)),
            dma((CHUNKS, STEPS)),
            dma((2,)),
            dma((2,)),
            dma((4 * REACH + 1,)),
            dma((4 * REACH + 1,)),
            dma((4 * REACH + 1,)),
            dma((4 * REACH + 1,)),
            dma((2,)),
            dma((2,)),
            pltpu.SemaphoreType.REGULAR((REACH - 1, 2)),
        ],
        compiler_params=pltpu.CompilerParams(
            collective_id=0, has_side_effects=True, vmem_limit_bytes=48 * 1024 * 1024
        ),
    )(
        *(pltpu.with_memory_space_constraint(a, pltpu.HBM) for a in (
            tokens.reshape(TOK, D),
            norm_gain.reshape(1, D),
            qkv_weight,
            out_weight,
            decode_weight.T,
            edges.transpose(0, 2, 1),
            truth.transpose(1, 2, 0),
        ))
    )
    return score, grad.reshape(1, V, 2, 64)


def solution(mesh):
    in_specs = (
        P("member", "mp", None, None),
        P(),
        P("mp", None),
        P("mp", None),
        P(),
        P("mp", None, None),
        P(None, "mp", "member"),
    )
    out_specs = (P("mp", "member"), P("member", None, "mp", None))
    return jax.shard_map(on_device, mesh=mesh, in_specs=in_specs, out_specs=out_specs, check_vma=False)
```
